512 devices in a mesh: dp: 32 (over y_hi, z), fsdp: 16 (over x, y_lo, core).
Axes of the slice: x: 4, y: 8 (y_hi: 4, y_lo: 2; y = y_hi * 2 + y_lo), z: 8, core: 2. Of those that a mesh axis runs over, the one named last changes fastest.
Arguments:
- queries: bfloat16 [16, 256, 4096], P('fsdp', 'dp'), may hold values from -0.125 to 0.125
- passages: bfloat16 [16, 256, 4096], P('fsdp', 'dp'), may hold values from -0.125 to 0.125
- positives: int32 [16, 256], P('fsdp', 'dp'), may hold values from 0 to 255, each once within a row
- hard_blocks: int32 [16, 256], P('fsdp', 'dp'), may hold values from 0 to 63
- residual: bfloat16 [16, 4096, 4096], P('fsdp', 'dp'), may hold values from -6 to 6
- hidden_act: bfloat16 [16, 4096, 14336], P('fsdp', 'dp'), may hold values from -6 to 6
- gain: bfloat16 [4096], replicated, may hold values from 0.099609375 to 1.8984375
- down_rows: bfloat16 [16, 14336], P(None, 'fsdp'), may hold values from -0.046875 to 0.046875
- up_weight_rows: bfloat16 [16, 4096], P(None, 'fsdp'), may hold values from -0.09375 to 0.09375
Outputs:
- query_grads: bfloat16 [16, 256, 4096], P('fsdp', 'dp')
- passage_grads: bfloat16 [16, 256, 4096], P('fsdp', 'dp')
- grad_down: float32 [16, 14336], P(None, 'fsdp')
- grad_up: float32 [16, 4096], P(None, 'fsdp')
The draws below stay inside these ranges and needn't reach their ends.
Inputs may be any that keep to these rules, and one draw needn't show every extreme that they name: `positives`: within each group every passage is the positive of exactly one query.
All inputs are finite; a program needn't handle non-finite values.
Results may differ from the reference program's by a relative error of at most 0.02.
Values may be sent and summed in bfloat16 or wider, within the bound.
A program may use at most 64 MiB of HBM per device.

```python
import jax
import jax.numpy as jnp
from jax import lax

D = 4096
HID = 14336
RANK = 16
HB = 4
Q_DEV = 8
LEN = 128
P_DEV = 8
GROUPS = 16
QG = 256
PG = 256
NBLK = 64
TOKS = 4096
N_DP = 32


def set_ends(entries, rng, low, high):
    longest = entries.shape.index(max(entries.shape))
    spots = []
    for shift in (0, 1):
        where = [jax.random.randint(jax.random.fold_in(rng, axis), (), 0, length) for axis, length in enumerate(entries.shape)]
        where[longest] = (where[longest] + shift) % entries.shape[longest]
        spots.append(tuple(where))
    return entries.at[spots[0]].set(low).at[spots[1]].set(high)


def level_of(key, extent, shards, low, high):
    def one(position, blocks):
        heights = jax.random.uniform(jax.random.fold_in(jax.random.fold_in(key, 6), position), (blocks,), jnp.float32, low / len(shards), high / len(shards))
        return jnp.repeat(jnp.exp(heights), extent[position] // blocks).reshape((-1,) + (1,) * (len(extent) - position - 1))

    loudness = one(*shards[0])
    for cut in shards[1:]:
        loudness = loudness * one(*cut)
    return loudness


def noise(own_key, extent, scale, reach, shards=(), kind=jnp.bfloat16):
    drawn = jax.random.normal(own_key, extent, jnp.float32) * scale
    if len(shards) > 0:
        drawn = level_of(own_key, extent, shards, -0.22, 0.18) * drawn
    return jnp.clip(drawn, min=-reach, max=reach).astype(kind)


def setup_inputs(seed: int = 0) -> dict:
    streams_of = jax.random.split(jax.random.key(seed), 10)
    queries = noise(streams_of[0], (GROUPS, QG, D), 0.02, 0.125, ((0, 16), (1, 32)))
    passages = noise(streams_of[1], (GROUPS, PG, D), 0.02, 0.125, ((0, 16), (1, 32)))
    positives = jax.vmap(lambda own: jax.random.permutation(own, PG))(jax.random.split(streams_of[2], GROUPS)).reshape((GROUPS, QG)).astype(jnp.int32)
    hard_blocks = set_ends(jax.random.randint(streams_of[3], (GROUPS, QG), 0, NBLK), jax.random.fold_in(streams_of[3], 1), 0, NBLK - 1).astype(jnp.int32)
    residual = noise(streams_of[4], (GROUPS, TOKS, D), 1.0, 6.0, ((0, 16), (1, 32)))
    hidden_act = noise(streams_of[5], (GROUPS, TOKS, HID), 1.0, 6.0, ((0, 16), (1, 32)))
    gain = jnp.clip(1.0 + 0.18 * jax.random.normal(streams_of[6], (D,), jnp.float32), 0.099609375, 1.8984375).astype(jnp.bfloat16)
    down_rows = noise(streams_of[7], (RANK, HID), HID ** -0.5, 0.046875, ((1, 16),))
    up_weight_rows = noise(streams_of[8], (RANK, D), D ** -0.5, 0.09375, ((1, 16),))
    return {"queries": queries, "passages": passages, "positives": positives, "hard_blocks": hard_blocks, "residual": residual, "hidden_act": hidden_act, "gain": gain, "down_rows": down_rows, "up_weight_rows": up_weight_rows}


inverse_warmth_factor = 50.0
difficult_distractor_extra = 1.3862943611198906
lowrank_scale = 2.0
norm_eps = 1e-06

def unit_rows(values):
    floats = values.astype(jnp.float32)
    length = jnp.sqrt(lax.optimization_barrier(jnp.sum(floats * floats, axis=-1, keepdims=True)) + norm_eps)
    return (floats / length, length)

def tangent(unit_vec, gradient, length):
    return (gradient - unit_vec * lax.optimization_barrier(jnp.sum(unit_vec * gradient, axis=-1, keepdims=True))) / length

def adapter_terms(residual_sequence, hidden_seq, upstream, gain, down_rows, up_weight_rows):
    seq_len = residual_sequence.shape[0]
    reduced_values = jnp.dot(hidden_seq, down_rows.T, preferred_element_type=jnp.float32).astype(jnp.bfloat16)
    residual_flow = residual_sequence.astype(jnp.float32) + lowrank_scale * jnp.dot(reduced_values, up_weight_rows, preferred_element_type=jnp.float32)
    root_mean = jnp.sqrt(lax.optimization_barrier(jnp.mean(residual_flow * residual_flow, axis=-1, keepdims=True)) + norm_eps)
    normed = residual_flow / root_mean
    grad_norm = gain.astype(jnp.float32)[None, :] * upstream[None, :] / seq_len
    residual_flow_gradient = ((grad_norm - normed * lax.optimization_barrier(jnp.mean(grad_norm * normed, axis=-1, keepdims=True))) / root_mean).astype(jnp.bfloat16)
    up_weight_term = lowrank_scale * jnp.dot(reduced_values.T, residual_flow_gradient, preferred_element_type=jnp.float32)
    reduced_gradient = (lowrank_scale * jnp.dot(residual_flow_gradient, up_weight_rows.T, preferred_element_type=jnp.float32)).astype(jnp.bfloat16)
    term_down = jnp.dot(reduced_gradient.T, hidden_seq, preferred_element_type=jnp.float32)
    return (term_down, up_weight_term)

def one_group(packed):
    group_query, group_passage, group_pos, group_hard = packed
    unit_query, len_query = unit_rows(group_query)
    unit_passage, len_passage = unit_rows(group_passage)
    question_vector = unit_query.astype(jnp.bfloat16)
    document_vector = unit_passage.astype(jnp.bfloat16)
    passage_ids = jnp.arange(PG, dtype=jnp.int32)
    cosine_matrix = inverse_warmth_factor * jnp.dot(question_vector, document_vector.T, preferred_element_type=jnp.float32)
    difficult_distractor_indicator = (passage_ids[None, :] // HB == group_hard[:, None]).astype(jnp.float32)
    cosine_matrix = cosine_matrix + difficult_distractor_extra * difficult_distractor_indicator
    normalized_probabilities = jnp.exp(cosine_matrix)
    softmax_rows = normalized_probabilities / lax.optimization_barrier(jnp.sum(normalized_probabilities, axis=1, keepdims=True))
    target = (passage_ids[None, :] == group_pos[:, None]).astype(jnp.float32)
    multiplier_factors = (softmax_rows - target).astype(jnp.bfloat16)
    factor_along_axis = multiplier_factors.reshape(QG, N_DP, P_DEV).astype(jnp.float32)
    documents_each_shard = document_vector.reshape(N_DP, P_DEV, D).astype(jnp.float32)
    question_share = inverse_warmth_factor * jnp.einsum('akh,khb->kab', factor_along_axis, documents_each_shard, precision=lax.Precision.HIGHEST)
    query_rounded = lax.optimization_barrier(question_share.astype(jnp.bfloat16))
    query_raw = lax.optimization_barrier(jnp.sum(query_rounded.astype(jnp.float32), axis=0))
    query_full = tangent(unit_query, query_raw, len_query)
    factor_on_shard = multiplier_factors.reshape(N_DP, Q_DEV, PG).astype(jnp.float32)
    vector_on_shard = question_vector.reshape(N_DP, Q_DEV, D).astype(jnp.float32)
    incomplete_amount = inverse_warmth_factor * jnp.einsum('ugc,ugo->uco', factor_on_shard, vector_on_shard, precision=lax.Precision.HIGHEST)
    rounded = lax.optimization_barrier(incomplete_amount.astype(jnp.bfloat16))
    passage_raw = lax.optimization_barrier(jnp.sum(rounded.astype(jnp.float32), axis=0))
    passage_full = tangent(unit_passage, passage_raw, len_passage)
    first_rows = query_full.reshape(N_DP, Q_DEV, D)[:, 0, :]
    return (query_full.astype(jnp.bfloat16), passage_full.astype(jnp.bfloat16), first_rows)

def reference(queries, passages, positives, hard_blocks, residual, hidden_act, gain, down_rows, up_weight_rows):
    query_grads, passage_grads, upstream = lax.map(one_group, (queries, passages, positives, hard_blocks))
    resid_all = residual.reshape(GROUPS * N_DP, LEN, D)
    hidden_all = hidden_act.reshape(GROUPS * N_DP, LEN, HID)
    upstream_all = upstream.reshape(GROUPS * N_DP, D)

    def accumulate(carry, packed):
        term_down, up_weight_term = adapter_terms(packed[0], packed[1], packed[2], gain, down_rows, up_weight_rows)
        return ((carry[0] + term_down, carry[1] + up_weight_term), None)
    start = (jnp.zeros((RANK, HID), jnp.float32), jnp.zeros((RANK, D), jnp.float32))
    totals, unused = lax.scan(accumulate, start, (resid_all, hidden_all, upstream_all))
    return (query_grads, passage_grads, totals[0], totals[1])
```

```python
import functools

import jax
import jax.numpy as jnp
from jax import lax
from jax.experimental import pallas as pl
from jax.experimental.pallas import tpu as pltpu
from jax.sharding import PartitionSpec as P

HB = 4
NZ = 8
SCALE = 50.0
EXTRA = 1.3862943611198906
EPS = 1e-06
F32 = jnp.float32
BF16 = jnp.bfloat16
MESH = pl.DeviceIdType.MESH


def dot(a, b, ca=1, cb=0):
    return lax.dot_general(a, b, (((ca,), (cb,)), ((), ())), preferred_element_type=F32)


def landed(ref, sem):
    pltpu.make_async_copy(ref, ref, sem).wait()


def loop(low, high, body):
    def step(k, carry):
        body(k)
        return carry

    lax.fori_loop(low, high, step, 0)


def as_column(row):
    n = row.shape[1]
    wide = jnp.broadcast_to(row, (n, n))
    eye = lax.broadcasted_iota(jnp.int32, (n, n), 0) == lax.broadcasted_iota(jnp.int32, (n, n), 1)
    return jnp.sum(jnp.where(eye, wide, 0.0), axis=1, keepdims=True)


def as_row(column):
    n = column.shape[0]
    wide = jnp.broadcast_to(column, (n, n))
    eye = lax.broadcasted_iota(jnp.int32, (n, n), 0) == lax.broadcasted_iota(jnp.int32, (n, n), 1)
    return jnp.sum(jnp.where(eye, wide, 0.0), axis=0, keepdims=True)


def split_rows(ref):
    wide = ref[...].astype(F32)
    n, _, w = wide.shape
    return [wide[:, 8 * h : 8 * h + 8, :].reshape(8 * n, w).astype(BF16) for h in (0, 1)]


def stacked(block):
    half = block.shape[-1] // 2
    return jnp.concatenate([block[:, :half], block[:, half:]], axis=0)


def kernel(
    ndp, nf,
    q_in, p_in, pos_in, hard_in, gain_in, down_in, up_in, res_hbm, hid_hbm,
    qg_out, pg_out, gd_out, gu_out,
    hid, res, normed, unit_q, unit_p, gain_row,
    eq, ep, rq, rp, pmat, qmat, ps, rs, rc, qs, rqr, pgs, rpg,
    rw, upf, sm, rmate, sa, ra, tiles, rb, rt,
    sem, msem, asem,
):
    nz = NZ
    ni = nf // 2
    rank, dw = down_in.shape
    uw = up_in.shape[1]
    sw = dw + uw
    d_model = unit_q.shape[1]
    fb = d_model // nz
    hw = fb // 2
    seq = res.shape[0]
    pg = ndp * 8
    n_tiles = tiles.shape[0]
    nc = sw // 128

    d = lax.axis_index("dp")
    f = lax.axis_index("fsdp")
    y, z = lax.div(d, nz), lax.rem(d, nz)
    i0, core = lax.div(f, 2), lax.rem(f, 2)
    mate = (d, 2 * i0 + 1 - core)

    def at_z(tz):
        return (y * nz + tz, f)

    def at_i(i):
        return (d, 2 * i + core)

    def send(src, dst, send_sem, recv_sem, device):
        pltpu.make_async_remote_copy(
            src_ref=src, dst_ref=dst, send_sem=send_sem, recv_sem=recv_sem,
            device_id=device, device_id_type=MESH,
        ).start()

    load_hid = pltpu.make_async_copy(hid_hbm.at[0], hid, sem.at[0])
    load_res = pltpu.make_async_copy(res_hbm.at[0], res, sem.at[1])
    load_hid.start()
    load_res.start()

    barrier = pltpu.get_barrier_semaphore()

    def greet(device):
        pl.semaphore_signal(barrier, inc=1, device_id=device, device_id_type=MESH)

    loop(1, ndp, lambda k: greet((lax.rem(d + k, ndp), f)))
    loop(1, ni, lambda k: greet(at_i(lax.rem(i0 + k, ni))))
    greet(mate)

    def unit_rows(ref, unit_ref, blocks):
        rows = ref[0].astype(F32)
        length = jnp.sqrt(jnp.sum(rows * rows, axis=1, keepdims=True) + EPS)
        unit = rows / length
        unit_ref[...] = unit
        for k in range(nz):
            blocks[k] = stacked(unit[:, k * fb : (k + 1) * fb]).astype(BF16)
        return length

    len_p = unit_rows(p_in, unit_p, ep)
    len_q = unit_rows(q_in, unit_q, eq)
    rp[d] = ep[z]
    rq[z] = eq[z]
    rw[core, i0] = jnp.concatenate([down_in[...], up_in[...]], axis=1)

    pl.semaphore_wait(barrier, (ndp - 1) + (ni - 1) + 1)

    def send_p(k):
        t = lax.rem(d + k, ndp)
        send(ep.at[lax.rem(t, nz)], rp.at[d], sem.at[2], sem.at[3], (t, f))

    def send_q(k):
        tz = lax.rem(z + k, nz)
        send(eq.at[tz], rq.at[z], sem.at[4], sem.at[5], at_z(tz))

    def send_w(k):
        i = lax.rem(i0 + k, ni)
        send(rw.at[core, i0], rw.at[core, i0], sem.at[6], sem.at[7], at_i(i))

    loop(1, ndp, send_p)
    loop(1, nz, send_q)
    loop(1, ni, send_w)

    for k in range(gain_in.shape[0]):
        gain_row[0:1, 128 * k : 128 * (k + 1)] = gain_in[...].astype(F32)[k : k + 1, :]

    landed(rq.at[pl.ds(0, nz - 1)], sem.at[5])
    landed(rp.at[pl.ds(0, ndp - 1)], sem.at[3])
    for h, half in enumerate(split_rows(rp)):
        pmat[h] = half
    for h, half in enumerate(split_rows(rq)):
        qmat[h] = half
    partial = dot(qmat[0], pmat[0], 1, 1) + dot(qmat[1], pmat[1], 1, 1)
    ps[...] = partial.reshape(nz, 8, pg)
    rs[z] = ps[z]

    def send_s(k):
        tz = lax.rem(z + k, nz)
        send(ps.at[tz], rs.at[z], sem.at[8], sem.at[9], at_z(tz))

    loop(1, nz, send_s)

    landed(rw.at[core, pl.ds(0, ni - 1)], sem.at[7])
    send(rw.at[core], rw.at[core], sem.at[10], sem.at[11], mate)
    load_hid.wait()

    def reduce_part(c, start):
        def step(i, acc):
            cols = pl.ds(pl.multiple_of((2 * i + c) * dw, 128), dw)
            return acc + dot(rw[c, i][:, :dw], hid[:, cols], 1, 1)

        return lax.fori_loop(0, ni, step, start)

    reduced_t = reduce_part(core, jnp.zeros((rank, seq), F32))

    landed(rs.at[pl.ds(0, nz - 1)], sem.at[9])
    ids = lax.broadcasted_iota(jnp.int32, (8, pg), 1)
    pos = as_column(pos_in[...].astype(F32))
    hard = as_column(hard_in[...].astype(F32))
    blocks = lax.shift_right_logical(ids, 2).astype(F32)
    logits = SCALE * jnp.sum(rs[...], axis=0) + jnp.where(blocks == hard, EXTRA, 0.0)
    weights = jnp.exp(logits)
    soft = weights / jnp.sum(weights, axis=1, keepdims=True)
    coeffs = soft - jnp.where(ids.astype(F32) == pos, 1.0, 0.0)
    rc[z] = stacked(coeffs).astype(BF16)

    def send_c(k):
        send(rc.at[z], rc.at[z], sem.at[12], sem.at[13], at_z(lax.rem(z + k, nz)))

    loop(1, nz, send_c)

    landed(rw.at[1 - core], sem.at[11])
    reduced_t = reduce_part(1 - core, reduced_t).astype(BF16)
    for c in range(2):
        for i in range(ni):
            at = (2 * i + c) * uw
            upf[:, at : at + uw] = rw[c, i][:, dw:]

    landed(rc.at[pl.ds(0, nz - 1)], sem.at[13])
    cmat = jnp.concatenate(split_rows(rc), axis=1)
    for h in range(2):
        qs[:, :, h * hw : (h + 1) * hw] = (SCALE * dot(cmat, pmat[h])).reshape(nz, 8, hw)
    rqr[z] = qs[z]

    def send_qr(k):
        tz = lax.rem(z + k, nz)
        send(qs.at[tz], rqr.at[z], sem.at[14], sem.at[15], at_z(tz))

    loop(1, nz, send_qr)
    terms = [(SCALE * dot(cmat, qmat[h], 0, 0)).reshape(ndp, 8, hw) for h in range(2)]
    pgs[...] = jnp.concatenate(terms, axis=1).astype(BF16)
    rpg[d] = pgs[d]

    def send_pg(k):
        t = lax.rem(d + k, ndp)
        send(pgs.at[t], rpg.at[d], sem.at[16], sem.at[17], (t, f))

    loop(1, ndp, send_pg)

    load_res.wait()
    cw = 512 if d_model % 512 == 0 else 128
    reduced = reduced_t.astype(F32).T.astype(BF16)

    def forward(j, squares):
        cols = pl.ds(pl.multiple_of(j * cw, 128), cw)
        part = res[:, cols].astype(F32) + 2.0 * dot(reduced, upf[:, cols])
        normed[:, cols] = part
        return squares + jnp.sum(part * part, axis=1, keepdims=True)

    squares = lax.fori_loop(0, d_model // cw, forward, jnp.zeros((seq, 1), F32))
    inv_root = 1.0 / jnp.sqrt(squares / d_model + EPS)
    inv_row = as_row(inv_root)

    def normalize(j, acc):
        cols = pl.ds(pl.multiple_of(j * cw, 128), cw)
        part = normed[:, cols] * inv_root
        normed[:, cols] = part
        high = part.astype(BF16)
        low = (part - high.astype(F32)).astype(BF16)
        return acc + (dot(upf[:, cols], high, 1, 1) + dot(upf[:, cols], low, 1, 1))

    normed_up = lax.fori_loop(0, d_model // cw, normalize, jnp.zeros((rank, seq), F32))

    landed(rqr.at[pl.ds(0, nz - 1)], sem.at[15])

    def tangent(unit_ref, pieces, length, out_ref):
        raw = jnp.concatenate(pieces, axis=1)
        unit = unit_ref[...]
        full = (raw - unit * jnp.sum(unit * raw, axis=1, keepdims=True)) / length
        out_ref[0] = full.astype(BF16)
        return full

    query_full = tangent(unit_q, [rqr[k] for k in range(nz)], len_q, qg_out)

    grad_norm = gain_row[...] * query_full[0:1, :] * (1.0 / seq)
    projected = jnp.sum(normed[...] * grad_norm, axis=1, keepdims=True) * (1.0 / d_model)
    up_grad = jnp.sum(upf[...].astype(F32) * grad_norm, axis=1, keepdims=True)
    grad_reduced_t = (2.0 * (up_grad - as_row(projected) * normed_up) * inv_row).astype(BF16)

    def terms_of(i, c):
        owner = 2 * i + c
        down_cols = pl.ds(pl.multiple_of(owner * dw, 128), dw)
        up_cols = pl.ds(pl.multiple_of(owner * uw, 128), uw)
        down_term = dot(grad_reduced_t, hid[:, down_cols])
        stream = ((gn[:, up_cols] - normed[:, up_cols] * projected) * inv_root).astype(BF16)
        return down_term, 2.0 * dot(reduced_t, stream)

    gn = gain_row
    gn[...] = grad_norm

    def for_mate(i):
        down_term, up_term = terms_of(i, 1 - core)
        sm[i, :, :dw] = down_term.astype(BF16)
        sm[i, :, dw:] = up_term.astype(BF16)
        send(sm.at[i], rmate.at[i], sem.at[18], msem.at[i], mate)

    def mate_step(k):
        for_mate(lax.rem(i0 + k, ni))

    loop(1, ni + 1, mate_step)

    def own_terms(i, out_ref, out_at):
        down_term, up_term = terms_of(i, core)
        landed(rmate.at[i], msem.at[i])
        other = rmate[i].astype(F32)
        out_ref[out_at, :, :dw] = (down_term + other[:, :dw]).astype(BF16)
        out_ref[out_at, :, dw:] = (up_term + other[:, dw:]).astype(BF16)

    def own_step(k):
        i = lax.rem(i0 + k, ni)
        own_terms(i, sa, i)
        send(sa.at[i], ra.at[i0], sem.at[19], sem.at[20], at_i(i))

    loop(1, ni, own_step)
    own_terms(i0, ra, i0)

    landed(ra.at[pl.ds(0, ni - 1)], sem.at[20])
    total = jnp.sum(ra[...].astype(F32), axis=0)
    for k in range(n_tiles):
        h, c = k // nc, k % nc
        tiles[k] = total[8 * h : 8 * h + 8, 128 * c : 128 * c + 128]

    own_tile = lax.div(d * n_tiles + ndp - 1, ndp)
    is_owner = (lax.div(own_tile * ndp, n_tiles) == d) & (own_tile < n_tiles)

    def send_tile(k):
        t = lax.div(k * ndp, n_tiles)

        @pl.when(t != d)
        def _():
            send(tiles.at[k], rb.at[d], sem.at[21], sem.at[22], (t, f))

    loop(0, n_tiles, send_tile)

    landed(rpg.at[pl.ds(0, ndp - 1)], sem.at[17])
    pieces = []
    for k in range(nz):
        both = rpg[k].astype(F32)
        for a in range(1, ndp // nz):
            both = both + rpg[a * nz + k].astype(F32)
        pieces += [both[:8], both[8:]]
    tangent(unit_p, pieces, len_p, pg_out)

    @pl.when(is_owner)
    def _():
        rb[d] = tiles[own_tile]
        landed(rb.at[pl.ds(0, ndp - 1)], sem.at[22])
        rt[own_tile] = jnp.sum(rb[...], axis=0)

        def send_total(k):
            t = lax.rem(d + k, ndp)
            send(rt.at[own_tile], rt.at[own_tile], sem.at[23], sem.at[24], (t, f))

        loop(1, ndp, send_total)
        landed(rt.at[pl.ds(0, n_tiles - 1)], sem.at[24])

    @pl.when(jnp.logical_not(is_owner))
    def _():
        landed(rt, sem.at[24])

    for k in range(n_tiles):
        h, c = k // nc, k % nc
        if c < dw // 128:
            gd_out[8 * h : 8 * h + 8, 128 * c : 128 * c + 128] = rt[k]
        else:
            at = 128 * c - dw
            gu_out[8 * h : 8 * h + 8, at : at + 128] = rt[k]

    landed(rp.at[pl.ds(0, ndp - 1)], sem.at[2])
    landed(rq.at[pl.ds(0, nz - 1)], sem.at[4])
    landed(rw.at[0, pl.ds(0, ni - 1)], sem.at[6])
    landed(rs.at[pl.ds(0, nz - 1)], sem.at[8])
    landed(rw.at[0], sem.at[10])
    landed(rc.at[pl.ds(0, nz - 1)], sem.at[12])
    landed(rqr.at[pl.ds(0, nz - 1)], sem.at[14])
    landed(rpg.at[pl.ds(0, ndp - 1)], sem.at[16])
    landed(sm, sem.at[18])
    landed(sa.at[pl.ds(0, ni - 1)], sem.at[19])

    @pl.when(is_owner)
    def _():
        landed(tiles.at[pl.ds(0, n_tiles - 1)], sem.at[21])
        landed(rb.at[pl.ds(0, ndp - 1)], sem.at[23])

    @pl.when(jnp.logical_not(is_owner))
    def _():
        landed(tiles, sem.at[21])


def per_device(ndp, nf, queries, passages, positives, hard_blocks, residual, hidden_act, gain, down_rows, up_rows):
    d_model = queries.shape[2]
    seq, hid = hidden_act.shape[1:]
    rank, dw = down_rows.shape
    uw = up_rows.shape[1]
    sw = dw + uw
    ni = nf // 2
    fb = d_model // NZ
    hw = fb // 2
    pg = ndp * 8
    n_tiles = (rank // 8) * (sw // 128)
    vmem = pl.BlockSpec(memory_space=pltpu.VMEM)
    anywhere = pl.BlockSpec(memory_space=pl.ANY)
    return pl.pallas_call(
        functools.partial(kernel, ndp, nf),
        out_shape=(
            jax.ShapeDtypeStruct(queries.shape, BF16),
            jax.ShapeDtypeStruct(passages.shape, BF16),
            jax.ShapeDtypeStruct(down_rows.shape, F32),
            jax.ShapeDtypeStruct(up_rows.shape, F32),
        ),
        in_specs=[vmem] * 7 + [anywhere] * 2,
        out_specs=(vmem,) * 4,
        scratch_shapes=[
            pltpu.VMEM((seq, hid), BF16),
            pltpu.VMEM((seq, d_model), BF16),
            pltpu.VMEM((seq, d_model), F32),
            pltpu.VMEM((8, d_model), F32),
            pltpu.VMEM((8, d_model), F32),
            pltpu.VMEM((1, d_model), F32),
            pltpu.VMEM((NZ, 16, hw), BF16),
            pltpu.VMEM((NZ, 16, hw), BF16),
            pltpu.VMEM((NZ, 16, hw), BF16),
            pltpu.VMEM((ndp, 16, hw), BF16),
            pltpu.VMEM((2, pg, hw), BF16),
            pltpu.VMEM((2, 8 * NZ, hw), BF16),
            pltpu.VMEM((NZ, 8, pg), F32),
            pltpu.VMEM((NZ, 8, pg), F32),
            pltpu.VMEM((NZ, 16, pg // 2), BF16),
            pltpu.VMEM((NZ, 8, fb), F32),
            pltpu.VMEM((NZ, 8, fb), F32),
            pltpu.VMEM((ndp, 16, hw), BF16),
            pltpu.VMEM((ndp, 16, hw), BF16),
            pltpu.VMEM((2, ni, rank, sw), BF16),
            pltpu.VMEM((rank, d_model), BF16),
            pltpu.VMEM((ni, rank, sw), BF16),
            pltpu.VMEM((ni, rank, sw), BF16),
            pltpu.VMEM((ni, rank, sw), BF16),
            pltpu.VMEM((ni, rank, sw), BF16),
            pltpu.VMEM((n_tiles, 8, 128), F32),
            pltpu.VMEM((ndp, 8, 128), F32),
            pltpu.VMEM((n_tiles, 8, 128), F32),
            pltpu.SemaphoreType.DMA((25,)),
            pltpu.SemaphoreType.DMA((ni,)),
            pltpu.SemaphoreType.DMA((1,)),
        ],
        compiler_params=pltpu.CompilerParams(
            collective_id=0, has_side_effects=True, vmem_limit_bytes=40 * 1024 * 1024
        ),
        name="contrastive_adapter",
    )(
        queries, passages, positives, hard_blocks, gain.reshape(d_model // 128, 128),
        down_rows, up_rows, residual, hidden_act,
    )


def solution(mesh):
    wide = P("fsdp", "dp", None)
    in_specs = (
        wide, wide, P("fsdp", "dp"), P("fsdp", "dp"), wide, wide, P(), P(None, "fsdp"), P(None, "fsdp"),
    )
    out_specs = (wide, wide, P(None, "fsdp"), P(None, "fsdp"))
    body = functools.partial(per_device, mesh.shape["dp"], mesh.shape["fsdp"])
    return jax.shard_map(body, mesh=mesh, in_specs=in_specs, out_specs=out_specs, check_vma=False)
```

```python
import functools

import jax
import jax.numpy as jnp
from jax import lax
from jax.experimental import pallas as pl
from jax.experimental.pallas import tpu as pltpu
from jax.sharding import PartitionSpec as P

HB = 4
NZ = 8
SCALE = 50.0
EXTRA = 1.3862943611198906
EPS = 1e-06
VMEM_BYTES = 64 * 1024 * 1024
F32 = jnp.float32
BF16 = jnp.bfloat16
MESH = pl.DeviceIdType.MESH


def dot(a, b, ca=1, cb=0):
    return lax.dot_general(a, b, (((ca,), (cb,)), ((), ())), preferred_element_type=F32)


def landed(ref, sem):
    pltpu.make_async_copy(ref, ref, sem).wait()


def loop(low, high, body):
    def step(k, carry):
        body(k)
        return carry

    lax.fori_loop(low, high, step, 0)


def as_column(row):
    n = row.shape[1]
    wide = jnp.broadcast_to(row, (n, n))
    eye = lax.broadcasted_iota(jnp.int32, (n, n), 0) == lax.broadcasted_iota(jnp.int32, (n, n), 1)
    return jnp.sum(jnp.where(eye, wide, 0.0), axis=1, keepdims=True)


def as_row(column):
    n = column.shape[0]
    wide = jnp.broadcast_to(column, (n, n))
    eye = lax.broadcasted_iota(jnp.int32, (n, n), 0) == lax.broadcasted_iota(jnp.int32, (n, n), 1)
    return jnp.sum(jnp.where(eye, wide, 0.0), axis=0, keepdims=True)


def split_rows(ref):
    wide = ref[...].astype(F32)
    n, _, w = wide.shape
    return [wide[:, 8 * h : 8 * h + 8, :].reshape(8 * n, w).astype(BF16) for h in (0, 1)]


def stacked(block):
    half = block.shape[-1] // 2
    return jnp.concatenate([block[:, :half], block[:, half:]], axis=0)


def farthest_first(ny, nz):
    offsets = [(dy, dz) for dy in range(ny) for dz in range(nz) if dy or dz]
    return sorted(offsets, key=lambda o: -(2 * min(o[0], ny - o[0]) + min(o[1], nz - o[1])))


def kernel(
    ndp, nf,
    q_hbm, p_hbm, pos_hbm, hard_hbm, gain_hbm, down_hbm, up_hbm, res_hbm, hid_hbm,
    qg_hbm, pg_hbm, gd_hbm, gu_hbm,
    qg_out, pg_out, gd_out, gu_out, q_in, p_in, pos_in, hard_in, gain_in, hid, res, normed, unit_q, unit_p, gain_row,
    eq, ep, rq, rp, pmat, qmat, ps, rs, rc, qs, rqr, pgs, rpg,
    rw, upf, sm, rmate, sa, ra, tiles, rb, rt,
    sem, msem, in_sem, out_sem,
):
    nz = NZ
    ny = ndp // nz
    ni = nf // 2
    rank, dw = down_hbm.shape
    uw = up_hbm.shape[1]
    sw = dw + uw
    d_model = unit_q.shape[1]
    fb = d_model // nz
    hw = fb // 2
    seq = res.shape[0]
    pg = ndp * 8
    n_tiles = tiles.shape[0]
    nc = sw // 128

    d = lax.axis_index("dp")
    f = lax.axis_index("fsdp")
    y, z = lax.div(d, nz), lax.rem(d, nz)
    i0, core = lax.div(f, 2), lax.rem(f, 2)
    mate = (d, 2 * i0 + 1 - core)

    def at_z(tz):
        return (y * nz + tz, f)

    def at_i(i):
        return (d, 2 * i + core)

    def send(src, dst, send_sem, recv_sem, device):
        pltpu.make_async_remote_copy(
            src_ref=src, dst_ref=dst, send_sem=send_sem, recv_sem=recv_sem,
            device_id=device, device_id_type=MESH,
        ).start()

    started = []
    own_w = rw.at[core, i0]
    loads = [
        pltpu.make_async_copy(src, dst, in_sem.at[k])
        for k, (src, dst) in enumerate((
            (p_hbm, p_in), (q_hbm, q_in),
            (down_hbm, own_w.at[:, pl.ds(0, dw)]), (up_hbm, own_w.at[:, pl.ds(dw, uw)]),
            (gain_hbm, gain_in), (pos_hbm, pos_in), (hard_hbm, hard_in),
            (hid_hbm.at[0], hid), (res_hbm.at[0], res),
        ))
    ]
    load_p, load_q, load_down, load_up, load_gain, load_pos, load_hard, load_hid, load_res = loads
    for load in loads:
        load.start()

    barrier = pltpu.get_barrier_semaphore()

    def greet(device):
        pl.semaphore_signal(barrier, inc=1, device_id=device, device_id_type=MESH)

    loop(1, ndp, lambda k: greet((lax.rem(d + k, ndp), f)))
    loop(1, ni, lambda k: greet(at_i(lax.rem(i0 + k, ni))))
    greet(mate)

    def unit_rows(ref, unit_ref, blocks):
        rows = ref[0].astype(F32)
        length = jnp.sqrt(jnp.sum(rows * rows, axis=1, keepdims=True) + EPS)
        unit = rows / length
        unit_ref[...] = unit
        for k in range(nz):
            blocks[k] = stacked(unit[:, k * fb : (k + 1) * fb]).astype(BF16)
        return length

    load_p.wait()
    len_p = unit_rows(p_in, unit_p, ep)
    load_q.wait()
    len_q = unit_rows(q_in, unit_q, eq)
    rp[d] = ep[z]
    rq[z] = eq[z]
    load_down.wait()
    load_up.wait()

    pl.semaphore_wait(barrier, (ndp - 1) + (ni - 1) + 1)

    def send_p(dy, dz):
        tz = lax.rem(z + dz, nz)
        t = lax.rem(y + dy, ny) * nz + tz
        send(ep.at[tz], rp.at[d], sem.at[2], sem.at[3], (t, f))

    def send_q(k):
        tz = lax.rem(z + k, nz)
        send(eq.at[tz], rq.at[z], sem.at[4], sem.at[5], at_z(tz))

    def send_w(k):
        i = lax.rem(i0 + k, ni)
        send(rw.at[core, i0], rw.at[core, i0], sem.at[6], sem.at[7], at_i(i))

    for dy, dz in farthest_first(ny, nz):
        send_p(dy, dz)
    loop(1, nz, send_q)
    loop(1, ni, send_w)
    started += [
        (rp.at[pl.ds(0, ndp - 1)], sem.at[2]), (rq.at[pl.ds(0, nz - 1)], sem.at[4]),
        (rw.at[0, pl.ds(0, ni - 1)], sem.at[6]),
    ]

    load_gain.wait()
    load_pos.wait()
    load_hard.wait()
    for k in range(gain_in.shape[0]):
        gain_row[0:1, 128 * k : 128 * (k + 1)] = gain_in[...].astype(F32)[k : k + 1, :]

    landed(rw.at[core, pl.ds(0, ni - 1)], sem.at[7])
    send(rw.at[core], rw.at[core], sem.at[10], sem.at[11], mate)
    started.append((rw.at[0], sem.at[10]))
    load_hid.wait()

    def reduce_part(c, start):
        def step(i, acc):
            cols = pl.ds(pl.multiple_of((2 * i + c) * dw, 128), dw)
            return acc + dot(rw[c, i][:, :dw], hid[:, cols], 1, 1)

        return lax.fori_loop(0, ni, step, start)

    reduced_t = reduce_part(core, jnp.zeros((rank, seq), F32))
    landed(rw.at[1 - core], sem.at[11])
    reduced_t = reduce_part(1 - core, reduced_t).astype(BF16)
    for c in range(2):
        for i in range(ni):
            at = (2 * i + c) * uw
            upf[:, at : at + uw] = rw[c, i][:, dw:]

    landed(rq.at[pl.ds(0, nz - 1)], sem.at[5])
    landed(rp.at[pl.ds(0, ndp - 1)], sem.at[3])
    for h, half in enumerate(split_rows(rp)):
        pmat[h] = half
    for h, half in enumerate(split_rows(rq)):
        qmat[h] = half
    partial = dot(qmat[0], pmat[0], 1, 1) + dot(qmat[1], pmat[1], 1, 1)
    ps[...] = partial.reshape(nz, 8, pg)
    rs[z] = ps[z]

    def send_s(k):
        tz = lax.rem(z + k, nz)
        send(ps.at[tz], rs.at[z], sem.at[8], sem.at[9], at_z(tz))

    loop(1, nz, send_s)
    started.append((rs.at[pl.ds(0, nz - 1)], sem.at[8]))

    load_res.wait()
    cw = 512 if d_model % 512 == 0 else 128
    reduced = reduced_t.astype(F32).T.astype(BF16)

    def forward(j, squares):
        cols = pl.ds(pl.multiple_of(j * cw, 128), cw)
        part = res[:, cols].astype(F32) + 2.0 * dot(reduced, upf[:, cols])
        normed[:, cols] = part
        return squares + jnp.sum(part * part, axis=1, keepdims=True)

    squares = lax.fori_loop(0, d_model // cw, forward, jnp.zeros((seq, 1), F32))
    inv_root = 1.0 / jnp.sqrt(squares / d_model + EPS)
    inv_row = as_row(inv_root)

    landed(rs.at[pl.ds(0, nz - 1)], sem.at[9])
    ids = lax.broadcasted_iota(jnp.int32, (8, pg), 1)
    pos = as_column(pos_in[...].astype(F32))
    hard = as_column(hard_in[...].astype(F32))
    blocks = lax.shift_right_logical(ids, 2).astype(F32)
    logits = SCALE * jnp.sum(rs[...], axis=0) + jnp.where(blocks == hard, EXTRA, 0.0)
    weights = jnp.exp(logits)
    soft = weights / jnp.sum(weights, axis=1, keepdims=True)
    coeffs = soft - jnp.where(ids.astype(F32) == pos, 1.0, 0.0)
    rc[z] = stacked(coeffs).astype(BF16)

    def send_c(k):
        send(rc.at[z], rc.at[z], sem.at[12], sem.at[13], at_z(lax.rem(z + k, nz)))

    loop(1, nz, send_c)
    started.append((rc.at[pl.ds(0, nz - 1)], sem.at[12]))

    def normalize(j, acc):
        cols = pl.ds(pl.multiple_of(j * cw, 128), cw)
        part = normed[:, cols] * inv_root
        normed[:, cols] = part
        high = part.astype(BF16)
        low = (part - high.astype(F32)).astype(BF16)
        return acc + (dot(upf[:, cols], high, 1, 1) + dot(upf[:, cols], low, 1, 1))

    normed_up = lax.fori_loop(0, d_model // cw, normalize, jnp.zeros((rank, seq), F32))

    landed(rc.at[pl.ds(0, nz - 1)], sem.at[13])
    cmat = jnp.concatenate(split_rows(rc), axis=1)
    for h in range(2):
        qs[:, :, h * hw : (h + 1) * hw] = (SCALE * dot(cmat, pmat[h])).reshape(nz, 8, hw)
    rqr[z] = qs[z]

    def send_qr(k):
        tz = lax.rem(z + k, nz)
        send(qs.at[tz], rqr.at[z], sem.at[14], sem.at[15], at_z(tz))

    loop(1, nz, send_qr)
    started.append((rqr.at[pl.ds(0, nz - 1)], sem.at[14]))
    terms = [(SCALE * dot(cmat, qmat[h], 0, 0)).reshape(ndp, 8, hw) for h in range(2)]
    pgs[...] = jnp.concatenate(terms, axis=1).astype(BF16)
    rpg[d] = pgs[d]


    landed(rqr.at[pl.ds(0, nz - 1)], sem.at[15])

    def tangent(unit_ref, pieces, length, out_ref):
        raw = jnp.concatenate(pieces, axis=1)
        unit = unit_ref[...]
        full = (raw - unit * jnp.sum(unit * raw, axis=1, keepdims=True)) / length
        out_ref[0] = full.astype(BF16)
        return full

    stores = [
        pltpu.make_async_copy(src, dst, out_sem.at[k])
        for k, (src, dst) in enumerate(((qg_out, qg_hbm), (pg_out, pg_hbm), (gd_out, gd_hbm), (gu_out, gu_hbm)))
    ]
    query_full = tangent(unit_q, [rqr[k] for k in range(nz)], len_q, qg_out)
    stores[0].start()

    grad_norm = gain_row[...] * query_full[0:1, :] * (1.0 / seq)
    projected = jnp.sum(normed[...] * grad_norm, axis=1, keepdims=True) * (1.0 / d_model)
    up_grad = jnp.sum(upf[...].astype(F32) * grad_norm, axis=1, keepdims=True)
    grad_reduced_t = (2.0 * (up_grad - as_row(projected) * normed_up) * inv_row).astype(BF16)

    def terms_of(i, c):
        owner = 2 * i + c
        down_cols = pl.ds(pl.multiple_of(owner * dw, 128), dw)
        up_cols = pl.ds(pl.multiple_of(owner * uw, 128), uw)
        down_term = dot(grad_reduced_t, hid[:, down_cols])
        stream = ((gn[:, up_cols] - normed[:, up_cols] * projected) * inv_root).astype(BF16)
        return down_term, 2.0 * dot(reduced_t, stream)

    gn = gain_row
    gn[...] = grad_norm

    def for_mate(i):
        down_term, up_term = terms_of(i, 1 - core)
        sm[i, :, :dw] = down_term.astype(BF16)
        sm[i, :, dw:] = up_term.astype(BF16)
        send(sm.at[i], rmate.at[i], sem.at[18], msem.at[i], mate)

    def mate_step(k):
        for_mate(lax.rem(i0 + k, ni))

    loop(1, ni + 1, mate_step)
    started.append((sm, sem.at[18]))

    def own_terms(i, out_ref, out_at):
        down_term, up_term = terms_of(i, core)
        landed(rmate.at[i], msem.at[i])
        other = rmate[i].astype(F32)
        out_ref[out_at, :, :dw] = (down_term + other[:, :dw]).astype(BF16)
        out_ref[out_at, :, dw:] = (up_term + other[:, dw:]).astype(BF16)

    def own_step(k):
        i = lax.rem(i0 + k, ni)
        own_terms(i, sa, i)
        send(sa.at[i], ra.at[i0], sem.at[19], sem.at[20], at_i(i))

    loop(1, ni, own_step)
    started.append((sa.at[pl.ds(0, ni - 1)], sem.at[19]))
    own_terms(i0, ra, i0)

    def send_pg(k):
        t = lax.rem(d + k, ndp)
        send(pgs.at[t], rpg.at[d], sem.at[16], sem.at[17], (t, f))

    loop(1, ndp, send_pg)
    started.append((rpg.at[pl.ds(0, ndp - 1)], sem.at[16]))

    landed(ra.at[pl.ds(0, ni - 1)], sem.at[20])
    total = jnp.sum(ra[...].astype(F32), axis=0)
    for k in range(n_tiles):
        h, c = k // nc, k % nc
        tiles[k] = total[8 * h : 8 * h + 8, 128 * c : 128 * c + 128]

    own_tile = lax.div(d * n_tiles + ndp - 1, ndp)
    is_owner = (lax.div(own_tile * ndp, n_tiles) == d) & (own_tile < n_tiles)

    def send_tile(k):
        t = lax.div(k * ndp, n_tiles)

        @pl.when(t != d)
        def _():
            send(tiles.at[k], rb.at[d], sem.at[21], sem.at[22], (t, f))

    loop(0, n_tiles, send_tile)

    landed(rpg.at[pl.ds(0, ndp - 1)], sem.at[17])
    pieces = []
    for k in range(nz):
        both = rpg[k].astype(F32)
        for a in range(1, ndp // nz):
            both = both + rpg[a * nz + k].astype(F32)
        pieces += [both[:8], both[8:]]
    tangent(unit_p, pieces, len_p, pg_out)
    stores[1].start()

    @pl.when(is_owner)
    def _():
        rb[d] = tiles[own_tile]
        landed(rb.at[pl.ds(0, ndp - 1)], sem.at[22])
        rt[own_tile] = jnp.sum(rb[...], axis=0)

        def send_total(k):
            t = lax.rem(d + k, ndp)
            send(rt.at[own_tile], rt.at[own_tile], sem.at[23], sem.at[24], (t, f))

        loop(1, ndp, send_total)
        landed(rt.at[pl.ds(0, n_tiles - 1)], sem.at[24])

    @pl.when(jnp.logical_not(is_owner))
    def _():
        landed(rt, sem.at[24])

    for k in range(n_tiles):
        h, c = k // nc, k % nc
        if c < dw // 128:
            gd_out[8 * h : 8 * h + 8, 128 * c : 128 * c + 128] = rt[k]
        else:
            at = 128 * c - dw
            gu_out[8 * h : 8 * h + 8, at : at + 128] = rt[k]
    stores[2].start()
    stores[3].start()

    for ref, left in started:
        landed(ref, left)

    @pl.when(is_owner)
    def _():
        landed(tiles.at[pl.ds(0, n_tiles - 1)], sem.at[21])
        landed(rb.at[pl.ds(0, ndp - 1)], sem.at[23])

    @pl.when(jnp.logical_not(is_owner))
    def _():
        landed(tiles, sem.at[21])

    for store in stores:
        store.wait()


def store_kernel(*refs):
    sources, results, staged, sem = refs[:4], refs[4:8], refs[8:12], refs[12]
    loads = [pltpu.make_async_copy(sources[k], staged[k], sem.at[0, k]) for k in range(4)]
    stores = [pltpu.make_async_copy(staged[k], results[k], sem.at[1, k]) for k in range(4)]
    for load in loads:
        load.start()
    for load, store in zip(loads, stores):
        load.wait()
        store.start()
    for store in stores:
        store.wait()


def per_device(ndp, nf, queries, passages, positives, hard_blocks, residual, hidden_act, gain, down_rows, up_rows):
    d_model = queries.shape[2]
    seq, hid = hidden_act.shape[1:]
    rank, dw = down_rows.shape
    uw = up_rows.shape[1]
    sw = dw + uw
    ni = nf // 2
    fb = d_model // NZ
    hw = fb // 2
    pg = ndp * 8
    n_tiles = (rank // 8) * (sw // 128)
    hbm = pl.BlockSpec(memory_space=pltpu.HBM)
    results = pl.pallas_call(
        functools.partial(kernel, ndp, nf),
        out_shape=(
            jax.ShapeDtypeStruct(queries.shape, BF16),
            jax.ShapeDtypeStruct(passages.shape, BF16),
            jax.ShapeDtypeStruct(down_rows.shape, F32),
            jax.ShapeDtypeStruct(up_rows.shape, F32),
        ),
        in_specs=[hbm] * 9,
        out_specs=(hbm,) * 4,
        scratch_shapes=[
            pltpu.VMEM(queries.shape, BF16),
            pltpu.VMEM(passages.shape, BF16),
            pltpu.VMEM(down_rows.shape, F32),
            pltpu.VMEM(up_rows.shape, F32),
            pltpu.VMEM(queries.shape, BF16),
            pltpu.VMEM(passages.shape, BF16),
            pltpu.VMEM(positives.shape, jnp.int32),
            pltpu.VMEM(hard_blocks.shape, jnp.int32),
            pltpu.VMEM((d_model // 128, 128), BF16),
            pltpu.VMEM((seq, hid), BF16),
            pltpu.VMEM((seq, d_model), BF16),
            pltpu.VMEM((seq, d_model), F32),
            pltpu.VMEM((8, d_model), F32),
            pltpu.VMEM((8, d_model), F32),
            pltpu.VMEM((1, d_model), F32),
            pltpu.VMEM((NZ, 16, hw), BF16),
            pltpu.VMEM((NZ, 16, hw), BF16),
            pltpu.VMEM((NZ, 16, hw), BF16),
            pltpu.VMEM((ndp, 16, hw), BF16),
            pltpu.VMEM((2, pg, hw), BF16),
            pltpu.VMEM((2, 8 * NZ, hw), BF16),
            pltpu.VMEM((NZ, 8, pg), F32),
            pltpu.VMEM((NZ, 8, pg), F32),
            pltpu.VMEM((NZ, 16, pg // 2), BF16),
            pltpu.VMEM((NZ, 8, fb), F32),
            pltpu.VMEM((NZ, 8, fb), F32),
            pltpu.VMEM((ndp, 16, hw), BF16),
            pltpu.VMEM((ndp, 16, hw), BF16),
            pltpu.VMEM((2, ni, rank, sw), BF16),
            pltpu.VMEM((rank, d_model), BF16),
            pltpu.VMEM((ni, rank, sw), BF16),
            pltpu.VMEM((ni, rank, sw), BF16),
            pltpu.VMEM((ni, rank, sw), BF16),
            pltpu.VMEM((ni, rank, sw), BF16),
            pltpu.VMEM((n_tiles, 8, 128), F32),
            pltpu.VMEM((ndp, 8, 128), F32),
            pltpu.VMEM((n_tiles, 8, 128), F32),
            pltpu.SemaphoreType.DMA((25,)),
            pltpu.SemaphoreType.DMA((ni,)),
            pltpu.SemaphoreType.DMA((9,)),
            pltpu.SemaphoreType.DMA((4,)),
        ],
        compiler_params=pltpu.CompilerParams(
            collective_id=0, has_side_effects=True, vmem_limit_bytes=VMEM_BYTES
        ),
        name="contrastive_adapter",
    )(
        queries, passages, positives, hard_blocks, gain.reshape(d_model // 128, 128),
        down_rows, up_rows, residual, hidden_act,
    )
    return pl.pallas_call(
        store_kernel,
        out_shape=tuple(jax.ShapeDtypeStruct(r.shape, r.dtype) for r in results),
        in_specs=[hbm] * 4,
        out_specs=(hbm,) * 4,
        scratch_shapes=[pltpu.VMEM(r.shape, r.dtype) for r in results] + [pltpu.SemaphoreType.DMA((2, 4))],
        compiler_params=pltpu.CompilerParams(vmem_limit_bytes=VMEM_BYTES),
        name="store_results",
    )(*results)


def solution(mesh):
    wide = P("fsdp", "dp", None)
    in_specs = (
        wide, wide, P("fsdp", "dp"), P("fsdp", "dp"), wide, wide, P(), P(None, "fsdp"), P(None, "fsdp"),
    )
    out_specs = (wide, wide, P(None, "fsdp"), P(None, "fsdp"))
    body = functools.partial(per_device, mesh.shape["dp"], mesh.shape["fsdp"])
    return jax.shard_map(body, mesh=mesh, in_specs=in_specs, out_specs=out_specs, check_vma=False)
```

```python
import functools

import jax
import jax.numpy as jnp
from jax import lax
from jax.experimental import pallas as pl
from jax.experimental.pallas import tpu as pltpu
from jax.sharding import PartitionSpec as P

HB = 4
NZ = 8
SCALE = 50.0
EXTRA = 1.3862943611198906
EPS = 1e-06
VMEM_BYTES = 48 * 1024 * 1024
F32 = jnp.float32
BF16 = jnp.bfloat16
MESH = pl.DeviceIdType.MESH


def dot(a, b, ca=1, cb=0):
    return lax.dot_general(a, b, (((ca,), (cb,)), ((), ())), preferred_element_type=F32)


def landed(ref, sem):
    pltpu.make_async_copy(ref, ref, sem).wait()


def loop(low, high, body, unroll=1):
    def step(k, carry):
        body(k)
        return carry

    lax.fori_loop(low, high, step, 0, unroll=unroll)


def as_column(row):
    n = row.shape[1]
    wide = jnp.broadcast_to(row, (n, n))
    eye = lax.broadcasted_iota(jnp.int32, (n, n), 0) == lax.broadcasted_iota(jnp.int32, (n, n), 1)
    return jnp.sum(jnp.where(eye, wide, 0.0), axis=1, keepdims=True)


def as_row(column):
    n = column.shape[0]
    wide = jnp.broadcast_to(column, (n, n))
    eye = lax.broadcasted_iota(jnp.int32, (n, n), 0) == lax.broadcasted_iota(jnp.int32, (n, n), 1)
    return jnp.sum(jnp.where(eye, wide, 0.0), axis=0, keepdims=True)


def split_rows(ref):
    wide = ref[...].astype(F32)
    n, _, w = wide.shape
    return [wide[:, 8 * h : 8 * h + 8, :].reshape(8 * n, w).astype(BF16) for h in (0, 1)]


def stacked(block):
    half = block.shape[-1] // 2
    return jnp.concatenate([block[:, :half], block[:, half:]], axis=0)


def farthest_first(ny, nz):
    offsets = [(dy, dz) for dy in range(ny) for dz in range(nz) if dy or dz]
    return sorted(offsets, key=lambda o: -(2 * min(o[0], ny - o[0]) + min(o[1], nz - o[1])))


def kernel(
    ndp, nf,
    q_hbm, p_hbm, pos_hbm, hard_hbm, gain_hbm, down_hbm, up_hbm, res_hbm, hid_hbm,
    qg_out, pg_out, gd_out, gu_out,
    q_in, p_in, pos_in, hard_in, gain_in, hid, res, normed, unit_q, unit_p, gain_row,
    eq, ep, rq, rp, pmat, qmat, ps, rs, rtag, rsc, qc, rqc, rc, qs, rqr, pgs, rpg,
    rw, upf, sm, rmate, sa, ra, tiles, rb, rt,
    sem, msem, in_sem,
):
    nz = NZ
    ny = ndp // nz
    ni = nf // 2
    rank, dw = down_hbm.shape
    uw = up_hbm.shape[1]
    sw = dw + uw
    d_model = unit_q.shape[1]
    fb = d_model // nz
    hw = fb // 2
    seq = res.shape[0]
    pg = ndp * 8
    n_tiles = tiles.shape[0]
    nc = sw // 128

    d = lax.axis_index("dp")
    f = lax.axis_index("fsdp")
    y, z = lax.div(d, nz), lax.rem(d, nz)
    i0, core = lax.div(f, 2), lax.rem(f, 2)
    mate = (d, 2 * i0 + 1 - core)

    def at_z(tz):
        return (y * nz + tz, f)

    def at_i(i):
        return (d, 2 * i + core)

    def send(src, dst, send_sem, recv_sem, device):
        pltpu.make_async_remote_copy(
            src_ref=src, dst_ref=dst, send_sem=send_sem, recv_sem=recv_sem,
            device_id=device, device_id_type=MESH,
        ).start()

    started = []
    own_w = rw.at[core, i0]
    loads = [
        pltpu.make_async_copy(src, dst, in_sem.at[k])
        for k, (src, dst) in enumerate((
            (p_hbm, p_in), (q_hbm, q_in),
            (down_hbm, own_w.at[:, pl.ds(0, dw)]), (up_hbm, own_w.at[:, pl.ds(dw, uw)]),
            (gain_hbm, gain_in), (pos_hbm, pos_in), (hard_hbm, hard_in),
            (hid_hbm.at[0], hid), (res_hbm.at[0], res),
        ))
    ]
    load_p, load_q, load_down, load_up, load_gain, load_pos, load_hard, load_hid, load_res = loads
    load_p.start()
    load_q.start()

    barrier = pltpu.get_barrier_semaphore()

    def greet(device):
        pl.semaphore_signal(barrier, inc=1, device_id=device, device_id_type=MESH)

    for dy, dz in farthest_first(ny, nz):
        greet((lax.rem(y + dy, ny) * nz + lax.rem(z + dz, nz), f))
    loop(1, ni, lambda k: greet(at_i(lax.rem(i0 + k, ni))))
    greet(mate)
    for load in loads[2:]:
        load.start()

    def unit_rows(ref, unit_ref, blocks):
        rows = ref[0].astype(F32)
        length = jnp.sqrt(jnp.sum(rows * rows, axis=1, keepdims=True) + EPS)
        unit = rows / length
        unit_ref[...] = unit
        for k in range(nz):
            blocks[k] = stacked(unit[:, k * fb : (k + 1) * fb]).astype(BF16)
        return length

    load_p.wait()
    len_p = unit_rows(p_in, unit_p, ep)
    load_q.wait()
    len_q = unit_rows(q_in, unit_q, eq)
    rp[d] = ep[z]
    rq[z] = eq[z]
    load_down.wait()
    load_up.wait()
    load_pos.wait()
    load_hard.wait()
    pos = as_column(pos_in[...].astype(F32))
    hard = as_column(hard_in[...].astype(F32))
    tag = jnp.where(lax.broadcasted_iota(jnp.int32, (8, 128), 1) < 64, pos[0:1], hard[0:1])
    rtag[z] = jnp.where(lax.broadcasted_iota(jnp.int32, (8, 128), 0) == z, tag, 0.0)

    pl.semaphore_wait(barrier, (ndp - 1) + (ni - 1) + 1)

    def send_p(dy, dz):
        tz = lax.rem(z + dz, nz)
        t = lax.rem(y + dy, ny) * nz + tz
        send(ep.at[tz], rp.at[d], sem.at[2], sem.at[3], (t, f))

    def send_q(k):
        tz = lax.rem(z + k, nz)
        send(eq.at[tz], rq.at[z], sem.at[4], sem.at[5], at_z(tz))
        send(rtag.at[z], rtag.at[z], sem.at[25], sem.at[26], at_z(tz))

    def send_w(k):
        i = lax.rem(i0 + k, ni)
        send(rw.at[core, i0], rw.at[core, i0], sem.at[6], sem.at[7], at_i(i))

    for dy, dz in farthest_first(ny, nz):
        send_p(dy, dz)
    loop(1, nz, send_q)
    loop(1, ni, send_w)
    started += [
        (rtag.at[pl.ds(0, nz - 1)], sem.at[25]),
        (rp.at[pl.ds(0, ndp - 1)], sem.at[2]), (rq.at[pl.ds(0, nz - 1)], sem.at[4]),
        (rw.at[0, pl.ds(0, ni - 1)], sem.at[6]),
    ]

    load_gain.wait()
    for k in range(gain_in.shape[0]):
        gain_row[0:1, 128 * k : 128 * (k + 1)] = gain_in[...].astype(F32)[k : k + 1, :]

    landed(rw.at[core, pl.ds(0, ni - 1)], sem.at[7])
    send(rw.at[core], rw.at[core], sem.at[10], sem.at[11], mate)
    started.append((rw.at[0], sem.at[10]))
    load_hid.wait()

    def reduce_part(c, start):
        def step(i, acc):
            cols = pl.ds(pl.multiple_of((2 * i + c) * dw, 128), dw)
            return acc + dot(rw[c, i][:, :dw], hid[:, cols], 1, 1)

        return lax.fori_loop(0, ni, step, start)

    reduced_t = reduce_part(core, jnp.zeros((rank, seq), F32))
    landed(rw.at[1 - core], sem.at[11])
    reduced_t = reduce_part(1 - core, reduced_t).astype(BF16)
    for c in range(2):
        for i in range(ni):
            at = (2 * i + c) * uw
            upf[:, at : at + uw] = rw[c, i][:, dw:]

    landed(rq.at[pl.ds(0, nz - 1)], sem.at[5])
    landed(rtag.at[pl.ds(0, nz - 1)], sem.at[26])
    landed(rp.at[pl.ds(0, ndp - 1)], sem.at[3])
    for h, half in enumerate(split_rows(rp)):
        pmat[h] = half
    for h, half in enumerate(split_rows(rq)):
        qmat[h] = half
    partial = dot(qmat[0], pmat[0], 1, 1) + dot(qmat[1], pmat[1], 1, 1)
    ps[...] = partial.reshape(nz, 8, pg)
    rs[z] = ps[z]
    for k in range(nz):
        rsc[z, k : k + 1, :] = ps[k, 0:1, :]

    def send_sc(k):
        send(rsc.at[z], rsc.at[z], sem.at[27], sem.at[28], at_z(lax.rem(z + k, nz)))

    loop(1, nz, send_sc)
    started.append((rsc.at[pl.ds(0, nz - 1)], sem.at[27]))

    load_res.wait()
    cw = d_model // 4
    reduced = reduced_t.astype(F32).T.astype(BF16)

    def forward(j, squares):
        cols = pl.ds(pl.multiple_of(j * cw, 128), cw)
        part = res[:, cols].astype(F32) + 2.0 * dot(reduced, upf[:, cols])
        normed[:, cols] = part
        return squares + jnp.sum(part * part, axis=1, keepdims=True)

    squares = lax.fori_loop(0, d_model // cw, forward, jnp.zeros((seq, 1), F32))
    inv_root = 1.0 / jnp.sqrt(squares / d_model + EPS)
    inv_row = as_row(inv_root)

    def coefficients(products, positive, hard_block):
        ids = lax.broadcasted_iota(jnp.int32, products.shape, 1)
        blocks = lax.shift_right_logical(ids, 2).astype(F32)
        weights = jnp.exp(SCALE * products + jnp.where(blocks == hard_block, EXTRA, 0.0))
        soft = weights / jnp.sum(weights, axis=1, keepdims=True)
        return soft - jnp.where(ids.astype(F32) == positive, 1.0, 0.0)

    landed(rsc.at[pl.ds(0, nz - 1)], sem.at[28])
    tags = jnp.sum(rtag[...], axis=0)[:nz]
    first = coefficients(jnp.sum(rsc[...], axis=0), tags[:, 0:1], tags[:, 64:65]).astype(BF16)
    for h in range(2):
        term = SCALE * dot(first, pmat[h])
        for k in range(hw // 128):
            qc[:, h * (hw // 128) + k, :] = term[:, 128 * k : 128 * k + 128]
    rqc[z] = qc[z]

    def send_qc(k):
        tz = lax.rem(z + k, nz)
        send(qc.at[tz], rqc.at[z], sem.at[29], sem.at[30], at_z(tz))

    loop(1, nz, send_qc)
    started.append((rqc.at[pl.ds(0, nz - 1)], sem.at[29]))

    def send_s(k):
        tz = lax.rem(z + k, nz)
        send(ps.at[tz], rs.at[z], sem.at[8], sem.at[9], at_z(tz))

    loop(1, nz, send_s)
    started.append((rs.at[pl.ds(0, nz - 1)], sem.at[8]))

    def normalize(j, acc):
        cols = pl.ds(pl.multiple_of(j * cw, 128), cw)
        part = normed[:, cols] * inv_root
        normed[:, cols] = part
        high = part.astype(BF16)
        low = (part - high.astype(F32)).astype(BF16)
        return acc + (dot(upf[:, cols], high, 1, 1) + dot(upf[:, cols], low, 1, 1))

    normed_up = lax.fori_loop(0, d_model // cw, normalize, jnp.zeros((rank, seq), F32))

    def tangent(unit, raw, length):
        return (raw - unit * jnp.sum(unit * raw, axis=1, keepdims=True)) / length

    landed(rqc.at[pl.ds(0, nz - 1)], sem.at[30])
    first_raw = jnp.concatenate([rqc[k, c : c + 1, :] for k in range(nz) for c in range(fb // 128)], axis=1)
    upstream = tangent(unit_q[0:1, :], first_raw, len_q[0:1, :])

    grad_norm = gain_row[...] * upstream * (1.0 / seq)
    projected = jnp.sum(normed[...] * grad_norm, axis=1, keepdims=True) * (1.0 / d_model)
    up_grad = jnp.sum(upf[...].astype(F32) * grad_norm, axis=1, keepdims=True)
    grad_reduced_t = (2.0 * (up_grad - as_row(projected) * normed_up) * inv_row).astype(BF16)

    def terms_of(i, c):
        owner = 2 * i + c
        down_cols = pl.ds(pl.multiple_of(owner * dw, 128), dw)
        up_cols = pl.ds(pl.multiple_of(owner * uw, 128), uw)
        down_term = dot(grad_reduced_t, hid[:, down_cols])
        stream = ((gn[:, up_cols] - normed[:, up_cols] * projected) * inv_root).astype(BF16)
        return down_term, 2.0 * dot(reduced_t, stream)

    gn = gain_row
    gn[...] = grad_norm

    def for_mate(i):
        down_term, up_term = terms_of(i, 1 - core)
        sm[i, :, :dw] = down_term.astype(BF16)
        sm[i, :, dw:] = up_term.astype(BF16)
        send(sm.at[i], rmate.at[i], sem.at[18], msem.at[i], mate)

    def mate_step(k):
        for_mate(lax.rem(i0 + k, ni))

    loop(1, ni + 1, mate_step, unroll=ni)
    started.append((sm, sem.at[18]))

    def own_terms(i, out_ref, out_at):
        down_term, up_term = terms_of(i, core)
        landed(rmate.at[i], msem.at[i])
        other = rmate[i].astype(F32)
        out_ref[out_at, :, :dw] = (down_term + other[:, :dw]).astype(BF16)
        out_ref[out_at, :, dw:] = (up_term + other[:, dw:]).astype(BF16)

    def own_step(k):
        i = lax.rem(i0 + k, ni)
        own_terms(i, sa, i)
        send(sa.at[i], ra.at[i0], sem.at[19], sem.at[20], at_i(i))

    loop(1, ni, own_step, unroll=ni - 1)
    started.append((sa.at[pl.ds(0, ni - 1)], sem.at[19]))
    own_terms(i0, ra, i0)

    landed(rs.at[pl.ds(0, nz - 1)], sem.at[9])
    coeffs = coefficients(jnp.sum(rs[...], axis=0), pos, hard)
    rc[z] = stacked(coeffs).astype(BF16)

    def send_c(k):
        send(rc.at[z], rc.at[z], sem.at[12], sem.at[13], at_z(lax.rem(z + k, nz)))

    loop(1, nz, send_c)
    started.append((rc.at[pl.ds(0, nz - 1)], sem.at[12]))

    landed(ra.at[pl.ds(0, ni - 1)], sem.at[20])
    total = jnp.sum(ra[...].astype(F32), axis=0)
    for k in range(n_tiles):
        h, c = k // nc, k % nc
        tiles[k] = total[8 * h : 8 * h + 8, 128 * c : 128 * c + 128]

    own_tile = lax.div(d * n_tiles + ndp - 1, ndp)
    is_owner = (lax.div(own_tile * ndp, n_tiles) == d) & (own_tile < n_tiles)

    def send_tile(k):
        t = lax.div(k * ndp, n_tiles)

        @pl.when(t != d)
        def _():
            send(tiles.at[k], rb.at[d], sem.at[21], sem.at[22], (t, f))

    loop(0, n_tiles, send_tile)

    landed(rc.at[pl.ds(0, nz - 1)], sem.at[13])
    cmat = jnp.concatenate(split_rows(rc), axis=1)
    for h in range(2):
        qs[:, :, h * hw : (h + 1) * hw] = (SCALE * dot(cmat, pmat[h])).reshape(nz, 8, hw)
    rqr[z] = qs[z]

    def send_qr(k):
        tz = lax.rem(z + k, nz)
        send(qs.at[tz], rqr.at[z], sem.at[14], sem.at[15], at_z(tz))

    loop(1, nz, send_qr)
    started.append((rqr.at[pl.ds(0, nz - 1)], sem.at[14]))
    terms = [(SCALE * dot(cmat, qmat[h], 0, 0)).reshape(ndp, 8, hw) for h in range(2)]
    pgs[...] = jnp.concatenate(terms, axis=1).astype(BF16)
    rpg[d] = pgs[d]

    def send_pg(k):
        t = lax.rem(d + k, ndp)
        send(pgs.at[t], rpg.at[d], sem.at[16], sem.at[17], (t, f))

    loop(1, ndp, send_pg)
    started.append((rpg.at[pl.ds(0, ndp - 1)], sem.at[16]))

    @pl.when(is_owner)
    def _():
        rb[d] = tiles[own_tile]
        landed(rb.at[pl.ds(0, ndp - 1)], sem.at[22])
        rt[own_tile] = jnp.sum(rb[...], axis=0)

        for dy, dz in farthest_first(ny, nz):
            t = lax.rem(y + dy, ny) * nz + lax.rem(z + dz, nz)
            send(rt.at[own_tile], rt.at[own_tile], sem.at[23], sem.at[24], (t, f))


    landed(rqr.at[pl.ds(0, nz - 1)], sem.at[15])
    raw = jnp.concatenate([rqr[k] for k in range(nz)], axis=1)
    qg_out[0] = tangent(unit_q[...], raw, len_q).astype(BF16)

    landed(rpg.at[pl.ds(0, ndp - 1)], sem.at[17])
    pieces = []
    for k in range(nz):
        both = rpg[k].astype(F32)
        for a in range(1, ny):
            both = both + rpg[a * nz + k].astype(F32)
        pieces += [both[:8], both[8:]]
    pg_out[0] = tangent(unit_p[...], jnp.concatenate(pieces, axis=1), len_p).astype(BF16)

    @pl.when(is_owner)
    def _():
        landed(rt.at[pl.ds(0, n_tiles - 1)], sem.at[24])

    @pl.when(jnp.logical_not(is_owner))
    def _():
        landed(rt, sem.at[24])

    for k in range(n_tiles):
        h, c = k // nc, k % nc
        if c < dw // 128:
            gd_out[8 * h : 8 * h + 8, 128 * c : 128 * c + 128] = rt[k]
        else:
            at = 128 * c - dw
            gu_out[8 * h : 8 * h + 8, at : at + 128] = rt[k]

    for ref, left in started:
        landed(ref, left)

    @pl.when(is_owner)
    def _():
        landed(tiles.at[pl.ds(0, n_tiles - 1)], sem.at[21])
        landed(rb.at[pl.ds(0, ndp - 1)], sem.at[23])

    @pl.when(jnp.logical_not(is_owner))
    def _():
        landed(tiles, sem.at[21])


def store_kernel(*refs):
    sources, results, sem = refs[:4], refs[4:8], refs[8]
    stores = [pltpu.make_async_copy(sources[k], results[k], sem.at[k]) for k in range(4)]
    for store in stores:
        store.start()
    for store in stores:
        store.wait()


def per_device(ndp, nf, queries, passages, positives, hard_blocks, residual, hidden_act, gain, down_rows, up_rows):
    d_model = queries.shape[2]
    seq, hid = hidden_act.shape[1:]
    rank, dw = down_rows.shape
    uw = up_rows.shape[1]
    sw = dw + uw
    ni = nf // 2
    fb = d_model // NZ
    hw = fb // 2
    pg = ndp * 8
    n_tiles = (rank // 8) * (sw // 128)
    hbm = pl.BlockSpec(memory_space=pltpu.HBM)
    vmem = pl.BlockSpec(memory_space=pltpu.VMEM)
    operands = (
        queries, passages, positives, hard_blocks, gain.reshape(d_model // 128, 128),
        down_rows, up_rows, residual, hidden_act,
    )
    results = pl.pallas_call(
        functools.partial(kernel, ndp, nf),
        out_shape=(
            pltpu.VMEM(queries.shape, BF16),
            pltpu.VMEM(passages.shape, BF16),
            pltpu.VMEM(down_rows.shape, F32),
            pltpu.VMEM(up_rows.shape, F32),
        ),
        in_specs=[hbm] * 9,
        out_specs=(vmem,) * 4,
        scratch_shapes=[
            pltpu.VMEM(queries.shape, BF16),
            pltpu.VMEM(passages.shape, BF16),
            pltpu.VMEM(positives.shape, jnp.int32),
            pltpu.VMEM(hard_blocks.shape, jnp.int32),
            pltpu.VMEM((d_model // 128, 128), BF16),
            pltpu.VMEM((seq, hid), BF16),
            pltpu.VMEM((seq, d_model), BF16),
            pltpu.VMEM((seq, d_model), F32),
            pltpu.VMEM((8, d_model), F32),
            pltpu.VMEM((8, d_model), F32),
            pltpu.VMEM((1, d_model), F32),
            pltpu.VMEM((NZ, 16, hw), BF16),
            pltpu.VMEM((NZ, 16, hw), BF16),
            pltpu.VMEM((NZ, 16, hw), BF16),
            pltpu.VMEM((ndp, 16, hw), BF16),
            pltpu.VMEM((2, pg, hw), BF16),
            pltpu.VMEM((2, 8 * NZ, hw), BF16),
            pltpu.VMEM((NZ, 8, pg), F32),
            pltpu.VMEM((NZ, 8, pg), F32),
            pltpu.VMEM((NZ, 8, 128), F32),
            pltpu.VMEM((NZ, NZ, pg), F32),
            pltpu.VMEM((NZ, fb // 128, 128), F32),
            pltpu.VMEM((NZ, fb // 128, 128), F32),
            pltpu.VMEM((NZ, 16, pg // 2), BF16),
            pltpu.VMEM((NZ, 8, fb), F32),
            pltpu.VMEM((NZ, 8, fb), F32),
            pltpu.VMEM((ndp, 16, hw), BF16),
            pltpu.VMEM((ndp, 16, hw), BF16),
            pltpu.VMEM((2, ni, rank, sw), BF16),
            pltpu.VMEM((rank, d_model), BF16),
            pltpu.VMEM((ni, rank, sw), BF16),
            pltpu.VMEM((ni, rank, sw), BF16),
            pltpu.VMEM((ni, rank, sw), BF16),
            pltpu.VMEM((ni, rank, sw), BF16),
            pltpu.VMEM((n_tiles, 8, 128), F32),
            pltpu.VMEM((ndp, 8, 128), F32),
            pltpu.VMEM((n_tiles, 8, 128), F32),
            pltpu.SemaphoreType.DMA((31,)),
            pltpu.SemaphoreType.DMA((ni,)),
            pltpu.SemaphoreType.DMA((9,)),
        ],
        compiler_params=pltpu.CompilerParams(
            collective_id=0, has_side_effects=True, vmem_limit_bytes=VMEM_BYTES
        ),
        name="contrastive_adapter",
    )(*(pltpu.with_memory_space_constraint(x, pltpu.HBM) for x in operands))
    return pl.pallas_call(
        store_kernel,
        out_shape=tuple(jax.ShapeDtypeStruct(r.shape, r.dtype) for r in results),
        in_specs=[vmem] * 4,
        out_specs=(hbm,) * 4,
        scratch_shapes=[pltpu.SemaphoreType.DMA((4,))],
        name="store_results",
    )(*results)


def solution(mesh):
    wide = P("fsdp", "dp", None)
    in_specs = (
        wide, wide, P("fsdp", "dp"), P("fsdp", "dp"), wide, wide, P(), P(None, "fsdp"), P(None, "fsdp"),
    )
    out_specs = (wide, wide, P(None, "fsdp"), P(None, "fsdp"))
    body = functools.partial(per_device, mesh.shape["dp"], mesh.shape["fsdp"])
    return jax.shard_map(body, mesh=mesh, in_specs=in_specs, out_specs=out_specs, check_vma=False)
```

```python
import functools

import jax
import jax.numpy as jnp
from jax import lax
from jax.experimental import pallas as pl
from jax.experimental.pallas import tpu as pltpu
from jax.sharding import PartitionSpec as P

HB = 4
NZ = 8
SCALE = 50.0
EXTRA = 1.3862943611198906
EPS = 1e-06
VMEM_BYTES = 48 * 1024 * 1024
F32 = jnp.float32
BF16 = jnp.bfloat16
MESH = pl.DeviceIdType.MESH


def dot(a, b, ca=1, cb=0):
    return lax.dot_general(a, b, (((ca,), (cb,)), ((), ())), preferred_element_type=F32)


def landed(ref, sem):
    pltpu.make_async_copy(ref, ref, sem).wait()


def loop(low, high, body, unroll=1):
    def step(k, carry):
        body(k)
        return carry

    lax.fori_loop(low, high, step, 0, unroll=unroll)


def as_column(row):
    n = row.shape[1]
    wide = jnp.broadcast_to(row, (n, n))
    eye = lax.broadcasted_iota(jnp.int32, (n, n), 0) == lax.broadcasted_iota(jnp.int32, (n, n), 1)
    return jnp.sum(jnp.where(eye, wide, 0.0), axis=1, keepdims=True)


def as_row(column):
    n = column.shape[0]
    wide = jnp.broadcast_to(column, (n, n))
    eye = lax.broadcasted_iota(jnp.int32, (n, n), 0) == lax.broadcasted_iota(jnp.int32, (n, n), 1)
    return jnp.sum(jnp.where(eye, wide, 0.0), axis=0, keepdims=True)


def split_rows(ref):
    wide = ref[...].astype(F32)
    n, _, w = wide.shape
    return [wide[:, 8 * h : 8 * h + 8, :].reshape(8 * n, w).astype(BF16) for h in (0, 1)]


def stacked(block):
    half = block.shape[-1] // 2
    return jnp.concatenate([block[:, :half], block[:, half:]], axis=0)


def farthest_first(ny, nz):
    offsets = [(dy, dz) for dy in range(ny) for dz in range(nz) if dy or dz]
    return sorted(offsets, key=lambda o: -(2 * min(o[0], ny - o[0]) + min(o[1], nz - o[1])))


def kernel(
    ndp, nf,
    q_hbm, p_hbm, pos_hbm, hard_hbm, gain_hbm, down_hbm, up_hbm, res_hbm, hid_hbm,
    qg_out, pg_out, gd_out, gu_out,
    q_in, p_in, pos_in, hard_in, gain_in, hid, res, normed, unit_q, unit_p, gain_row,
    eq, ep, rq, rp, pmat, qmat, ps, rs, rtag, rsc, qc, rqc, rc, qs, rqr, pgs, rpg,
    rw, upf, sm, rmate, sa, ra, tiles, rb, rt,
    sem, msem, in_sem,
):
    nz = NZ
    ny = ndp // nz
    ni = nf // 2
    rank, dw = down_hbm.shape
    uw = up_hbm.shape[1]
    sw = dw + uw
    d_model = unit_q.shape[1]
    fb = d_model // nz
    hw = fb // 2
    seq = res.shape[0]
    pg = ndp * 8
    n_tiles = tiles.shape[0]
    nc = sw // 128

    d = lax.axis_index("dp")
    f = lax.axis_index("fsdp")
    y, z = lax.div(d, nz), lax.rem(d, nz)
    i0, core = lax.div(f, 2), lax.rem(f, 2)
    nx = ni // 2
    x, yl = lax.div(i0, 2), lax.rem(i0, 2)
    mate = (d, 2 * i0 + 1 - core)

    def at_z(tz):
        return (y * nz + tz, f)

    def at_i(i):
        return (d, 2 * i + core)

    def send(src, dst, send_sem, recv_sem, device):
        pltpu.make_async_remote_copy(
            src_ref=src, dst_ref=dst, send_sem=send_sem, recv_sem=recv_sem,
            device_id=device, device_id_type=MESH,
        ).start()

    started = []
    own_w = rw.at[core, yl, x]
    loads = [
        pltpu.make_async_copy(src, dst, in_sem.at[k])
        for k, (src, dst) in enumerate((
            (p_hbm, p_in), (q_hbm, q_in),
            (down_hbm, own_w.at[:, pl.ds(0, dw)]), (up_hbm, own_w.at[:, pl.ds(dw, uw)]),
            (gain_hbm, gain_in), (pos_hbm, pos_in), (hard_hbm, hard_in),
            (hid_hbm.at[0], hid), (res_hbm.at[0], res),
        ))
    ]
    load_p, load_q, load_down, load_up, load_gain, load_pos, load_hard, load_hid, load_res = loads
    load_p.start()
    load_q.start()

    barrier = pltpu.get_barrier_semaphore()

    def greet(device):
        pl.semaphore_signal(barrier, inc=1, device_id=device, device_id_type=MESH)

    for dy, dz in farthest_first(ny, nz):
        greet((lax.rem(y + dy, ny) * nz + lax.rem(z + dz, nz), f))
    loop(1, ni, lambda k: greet(at_i(lax.rem(i0 + k, ni))))
    greet(mate)
    for load in loads[2:]:
        load.start()

    def unit_rows(ref, unit_ref, blocks):
        rows = ref[0].astype(F32)
        length = jnp.sqrt(jnp.sum(rows * rows, axis=1, keepdims=True) + EPS)
        unit = rows / length
        unit_ref[...] = unit
        for k in range(nz):
            blocks[k] = stacked(unit[:, k * fb : (k + 1) * fb]).astype(BF16)
        return length

    load_p.wait()
    len_p = unit_rows(p_in, unit_p, ep)
    load_q.wait()
    len_q = unit_rows(q_in, unit_q, eq)
    rp[d] = ep[z]
    rq[z] = eq[z]
    load_down.wait()
    load_up.wait()
    load_pos.wait()
    load_hard.wait()
    pos = as_column(pos_in[...].astype(F32))
    hard = as_column(hard_in[...].astype(F32))
    tag = jnp.where(lax.broadcasted_iota(jnp.int32, (8, 128), 1) < 64, pos[0:1], hard[0:1])
    rtag[z] = jnp.where(lax.broadcasted_iota(jnp.int32, (8, 128), 0) == z, tag, 0.0)

    pl.semaphore_wait(barrier, (ndp - 1) + (ni - 1) + 1)

    def send_p(dy, dz):
        tz = lax.rem(z + dz, nz)
        t = lax.rem(y + dy, ny) * nz + tz
        send(ep.at[tz], rp.at[d], sem.at[2], sem.at[3], (t, f))

    def send_q(k):
        tz = lax.rem(z + k, nz)
        send(eq.at[tz], rq.at[z], sem.at[4], sem.at[5], at_z(tz))
        send(rtag.at[z], rtag.at[z], sem.at[25], sem.at[26], at_z(tz))

    def send_w(k):
        send(own_w, own_w, sem.at[6], sem.at[7], at_i(2 * lax.rem(x + k, nx) + yl))

    for dy, dz in farthest_first(ny, nz):
        send_p(dy, dz)
    loop(1, nz, send_q)
    loop(1, nx, send_w)
    started += [
        (rtag.at[pl.ds(0, nz - 1)], sem.at[25]),
        (rp.at[pl.ds(0, ndp - 1)], sem.at[2]), (rq.at[pl.ds(0, nz - 1)], sem.at[4]),
    ]
    if nx > 1:
        started.append((rw.at[0, 0, pl.ds(0, nx - 1)], sem.at[6]))

    load_gain.wait()
    for k in range(gain_in.shape[0]):
        gain_row[0:1, 128 * k : 128 * (k + 1)] = gain_in[...].astype(F32)[k : k + 1, :]

    if nx > 1:
        landed(rw.at[core, yl, pl.ds(0, nx - 1)], sem.at[7])
    send(rw.at[core, yl], rw.at[core, yl], sem.at[10], sem.at[11], mate)
    started.append((rw.at[0, 0], sem.at[10]))
    load_hid.wait()

    def reduce_part(c, row, start):
        def step(k, acc):
            cols = pl.ds(pl.multiple_of((4 * k + 2 * row + c) * dw, 128), dw)
            return acc + dot(rw[c, row, k][:, :dw], hid[:, cols], 1, 1)

        return lax.fori_loop(0, nx, step, start, unroll=nx)

    reduced_t = reduce_part(core, yl, jnp.zeros((rank, seq), F32))
    landed(rw.at[1 - core, yl], sem.at[11])
    reduced_t = reduce_part(1 - core, yl, reduced_t)

    landed(rq.at[pl.ds(0, nz - 1)], sem.at[5])
    landed(rtag.at[pl.ds(0, nz - 1)], sem.at[26])
    landed(rp.at[pl.ds(0, ndp - 1)], sem.at[3])
    for h, half in enumerate(split_rows(rp)):
        pmat[h] = half
    for h, half in enumerate(split_rows(rq)):
        qmat[h] = half
    partial = dot(qmat[0], pmat[0], 1, 1) + dot(qmat[1], pmat[1], 1, 1)
    ps[...] = partial.reshape(nz, 8, pg)
    rs[z] = ps[z]
    for k in range(nz):
        rsc[z, k : k + 1, :] = ps[k, 0:1, :]

    def send_sc(k):
        send(rsc.at[z], rsc.at[z], sem.at[27], sem.at[28], at_z(lax.rem(z + k, nz)))

    loop(1, nz, send_sc)
    started.append((rsc.at[pl.ds(0, nz - 1)], sem.at[27]))

    send(rw.at[core, yl], rw.at[core, yl], sem.at[31], sem.at[32], at_i(2 * x + 1 - yl))
    started.append((rw.at[0, 0], sem.at[31]))
    landed(rw.at[core, 1 - yl], sem.at[32])
    send(rw.at[core, 1 - yl], rw.at[core, 1 - yl], sem.at[33], sem.at[34], mate)
    started.append((rw.at[0, 0], sem.at[33]))
    reduced_t = reduce_part(core, 1 - yl, reduced_t)

    def coefficients(products, positive, hard_block):
        ids = lax.broadcasted_iota(jnp.int32, products.shape, 1)
        blocks = lax.shift_right_logical(ids, 2).astype(F32)
        weights = jnp.exp(SCALE * products + jnp.where(blocks == hard_block, EXTRA, 0.0))
        soft = weights / jnp.sum(weights, axis=1, keepdims=True)
        return soft - jnp.where(ids.astype(F32) == positive, 1.0, 0.0)

    landed(rsc.at[pl.ds(0, nz - 1)], sem.at[28])
    tags = jnp.sum(rtag[...], axis=0)[:nz]
    first = coefficients(jnp.sum(rsc[...], axis=0), tags[:, 0:1], tags[:, 64:65]).astype(BF16)
    for h in range(2):
        term = SCALE * dot(first, pmat[h])
        for k in range(hw // 128):
            qc[:, h * (hw // 128) + k, :] = term[:, 128 * k : 128 * k + 128]
    rqc[z] = qc[z]

    def send_qc(k):
        tz = lax.rem(z + k, nz)
        send(qc.at[tz], rqc.at[z], sem.at[29], sem.at[30], at_z(tz))

    loop(1, nz, send_qc)
    started.append((rqc.at[pl.ds(0, nz - 1)], sem.at[29]))

    def send_s(k):
        tz = lax.rem(z + k, nz)
        send(ps.at[tz], rs.at[z], sem.at[8], sem.at[9], at_z(tz))

    loop(1, nz, send_s)
    started.append((rs.at[pl.ds(0, nz - 1)], sem.at[8]))

    landed(rw.at[1 - core, 1 - yl], sem.at[34])
    reduced_t = reduce_part(1 - core, 1 - yl, reduced_t).astype(BF16)
    for c in range(2):
        for row in range(2):
            for k in range(nx):
                at = (4 * k + 2 * row + c) * uw
                upf[:, at : at + uw] = rw[c, row, k][:, dw:]

    load_res.wait()
    cw = d_model // 4
    reduced = reduced_t.astype(F32).T.astype(BF16)

    def forward(j, squares):
        cols = pl.ds(pl.multiple_of(j * cw, 128), cw)
        part = res[:, cols].astype(F32) + 2.0 * dot(reduced, upf[:, cols])
        normed[:, cols] = part
        return squares + jnp.sum(part * part, axis=1, keepdims=True)

    squares = lax.fori_loop(0, d_model // cw, forward, jnp.zeros((seq, 1), F32))
    inv_root = 1.0 / jnp.sqrt(squares / d_model + EPS)
    inv_row = as_row(inv_root)

    def normalize(j, acc):
        cols = pl.ds(pl.multiple_of(j * cw, 128), cw)
        part = normed[:, cols] * inv_root
        normed[:, cols] = part
        high = part.astype(BF16)
        low = (part - high.astype(F32)).astype(BF16)
        return acc + (dot(upf[:, cols], high, 1, 1) + dot(upf[:, cols], low, 1, 1))

    normed_up = lax.fori_loop(0, d_model // cw, normalize, jnp.zeros((rank, seq), F32))

    def tangent(unit, raw, length):
        return (raw - unit * jnp.sum(unit * raw, axis=1, keepdims=True)) / length

    landed(rqc.at[pl.ds(0, nz - 1)], sem.at[30])
    first_raw = jnp.concatenate([rqc[k, c : c + 1, :] for k in range(nz) for c in range(fb // 128)], axis=1)
    upstream = tangent(unit_q[0:1, :], first_raw, len_q[0:1, :])

    grad_norm = gain_row[...] * upstream * (1.0 / seq)
    projected = jnp.sum(normed[...] * grad_norm, axis=1, keepdims=True) * (1.0 / d_model)
    up_grad = jnp.sum(upf[...].astype(F32) * grad_norm, axis=1, keepdims=True)
    grad_reduced_t = (2.0 * (up_grad - as_row(projected) * normed_up) * inv_row).astype(BF16)

    def terms_of(i, c):
        owner = 2 * i + c
        down_cols = pl.ds(pl.multiple_of(owner * dw, 128), dw)
        up_cols = pl.ds(pl.multiple_of(owner * uw, 128), uw)
        down_term = dot(grad_reduced_t, hid[:, down_cols])
        stream = ((gn[:, up_cols] - normed[:, up_cols] * projected) * inv_root).astype(BF16)
        return down_term, 2.0 * dot(reduced_t, stream)

    gn = gain_row
    gn[...] = grad_norm

    def for_mate(i):
        down_term, up_term = terms_of(i, 1 - core)
        sm[i, :, :dw] = down_term.astype(BF16)
        sm[i, :, dw:] = up_term.astype(BF16)
        send(sm.at[i], rmate.at[i], sem.at[18], msem.at[i], mate)

    def mate_step(k):
        for_mate(lax.rem(i0 + k, ni))

    loop(1, ni + 1, mate_step, unroll=ni)
    started.append((sm, sem.at[18]))

    def own_terms(i, out_ref, out_at):
        down_term, up_term = terms_of(i, core)
        landed(rmate.at[i], msem.at[i])
        other = rmate[i].astype(F32)
        out_ref[out_at, :, :dw] = (down_term + other[:, :dw]).astype(BF16)
        out_ref[out_at, :, dw:] = (up_term + other[:, dw:]).astype(BF16)

    def own_step(k):
        i = lax.rem(i0 + k, ni)
        own_terms(i, sa, i)
        send(sa.at[i], ra.at[i0], sem.at[19], sem.at[20], at_i(i))

    loop(1, ni, own_step, unroll=ni - 1)
    started.append((sa.at[pl.ds(0, ni - 1)], sem.at[19]))
    own_terms(i0, ra, i0)

    landed(rs.at[pl.ds(0, nz - 1)], sem.at[9])
    coeffs = coefficients(jnp.sum(rs[...], axis=0), pos, hard)
    rc[z] = stacked(coeffs).astype(BF16)

    def send_c(k):
        send(rc.at[z], rc.at[z], sem.at[12], sem.at[13], at_z(lax.rem(z + k, nz)))

    loop(1, nz, send_c)
    started.append((rc.at[pl.ds(0, nz - 1)], sem.at[12]))

    landed(ra.at[pl.ds(0, ni - 1)], sem.at[20])
    total = jnp.sum(ra[...].astype(F32), axis=0)
    for k in range(n_tiles):
        h, c = k // nc, k % nc
        tiles[k] = total[8 * h : 8 * h + 8, 128 * c : 128 * c + 128]

    own_tile = lax.div(d * n_tiles + ndp - 1, ndp)
    is_owner = (lax.div(own_tile * ndp, n_tiles) == d) & (own_tile < n_tiles)

    def send_tile(k):
        t = lax.div(k * ndp, n_tiles)

        @pl.when(t != d)
        def _():
            send(tiles.at[k], rb.at[d], sem.at[21], sem.at[22], (t, f))

    loop(0, n_tiles, send_tile)

    landed(rc.at[pl.ds(0, nz - 1)], sem.at[13])
    cmat = jnp.concatenate(split_rows(rc), axis=1)
    terms = [(SCALE * dot(cmat, pmat[h])).reshape(nz, 8, hw) for h in range(2)]
    qs[...] = jnp.concatenate(terms, axis=1).astype(BF16)
    rqr[z] = qs[z]

    def send_qr(k):
        tz = lax.rem(z + k, nz)
        send(qs.at[tz], rqr.at[z], sem.at[14], sem.at[15], at_z(tz))

    loop(1, nz, send_qr)
    started.append((rqr.at[pl.ds(0, nz - 1)], sem.at[14]))
    terms = [(SCALE * dot(cmat, qmat[h], 0, 0)).reshape(ndp, 8, hw) for h in range(2)]
    pgs[...] = jnp.concatenate(terms, axis=1).astype(BF16)
    rpg[d] = pgs[d]

    for dy, dz in farthest_first(ny, nz):
        t = lax.rem(y + dy, ny) * nz + lax.rem(z + dz, nz)
        send(pgs.at[t], rpg.at[d], sem.at[16], sem.at[17], (t, f))

    started.append((rpg.at[pl.ds(0, ndp - 1)], sem.at[16]))

    @pl.when(is_owner)
    def _():
        rb[d] = tiles[own_tile]
        landed(rb.at[pl.ds(0, ndp - 1)], sem.at[22])
        rt[own_tile] = jnp.sum(rb[...], axis=0)

        for dy, dz in farthest_first(ny, nz):
            t = lax.rem(y + dy, ny) * nz + lax.rem(z + dz, nz)
            send(rt.at[own_tile], rt.at[own_tile], sem.at[23], sem.at[24], (t, f))


    landed(rqr.at[pl.ds(0, nz - 1)], sem.at[15])
    pieces = []
    for k in range(nz):
        both = rqr[k].astype(F32)
        pieces += [both[:8], both[8:]]
    raw = jnp.concatenate(pieces, axis=1)
    qg_out[0] = tangent(unit_q[...], raw, len_q).astype(BF16)

    landed(rpg.at[pl.ds(0, ndp - 1)], sem.at[17])
    pieces = []
    for k in range(nz):
        both = rpg[k].astype(F32)
        for a in range(1, ny):
            both = both + rpg[a * nz + k].astype(F32)
        pieces += [both[:8], both[8:]]
    pg_out[0] = tangent(unit_p[...], jnp.concatenate(pieces, axis=1), len_p).astype(BF16)

    @pl.when(is_owner)
    def _():
        landed(rt.at[pl.ds(0, n_tiles - 1)], sem.at[24])

    @pl.when(jnp.logical_not(is_owner))
    def _():
        landed(rt, sem.at[24])

    for k in range(n_tiles):
        h, c = k // nc, k % nc
        if c < dw // 128:
            gd_out[8 * h : 8 * h + 8, 128 * c : 128 * c + 128] = rt[k]
        else:
            at = 128 * c - dw
            gu_out[8 * h : 8 * h + 8, at : at + 128] = rt[k]

    for ref, left in started:
        landed(ref, left)

    @pl.when(is_owner)
    def _():
        landed(tiles.at[pl.ds(0, n_tiles - 1)], sem.at[21])
        landed(rb.at[pl.ds(0, ndp - 1)], sem.at[23])

    @pl.when(jnp.logical_not(is_owner))
    def _():
        landed(tiles, sem.at[21])


def store_kernel(*refs):
    sources, results, sem = refs[:4], refs[4:8], refs[8]
    stores = [pltpu.make_async_copy(sources[k], results[k], sem.at[k]) for k in range(4)]
    for store in stores:
        store.start()
    for store in stores:
        store.wait()


def per_device(ndp, nf, queries, passages, positives, hard_blocks, residual, hidden_act, gain, down_rows, up_rows):
    d_model = queries.shape[2]
    seq, hid = hidden_act.shape[1:]
    rank, dw = down_rows.shape
    uw = up_rows.shape[1]
    sw = dw + uw
    ni = nf // 2
    fb = d_model // NZ
    hw = fb // 2
    pg = ndp * 8
    n_tiles = (rank // 8) * (sw // 128)
    hbm = pl.BlockSpec(memory_space=pltpu.HBM)
    vmem = pl.BlockSpec(memory_space=pltpu.VMEM)
    operands = (
        queries, passages, positives, hard_blocks, gain.reshape(d_model // 128, 128),
        down_rows, up_rows, residual, hidden_act,
    )
    results = pl.pallas_call(
        functools.partial(kernel, ndp, nf),
        out_shape=(
            pltpu.VMEM(queries.shape, BF16),
            pltpu.VMEM(passages.shape, BF16),
            pltpu.VMEM(down_rows.shape, F32),
            pltpu.VMEM(up_rows.shape, F32),
        ),
        in_specs=[hbm] * 9,
        out_specs=(vmem,) * 4,
        scratch_shapes=[
            pltpu.VMEM(queries.shape, BF16),
            pltpu.VMEM(passages.shape, BF16),
            pltpu.VMEM(positives.shape, jnp.int32),
            pltpu.VMEM(hard_blocks.shape, jnp.int32),
            pltpu.VMEM((d_model // 128, 128), BF16),
            pltpu.VMEM((seq, hid), BF16),
            pltpu.VMEM((seq, d_model), BF16),
            pltpu.VMEM((seq, d_model), F32),
            pltpu.VMEM((8, d_model), F32),
            pltpu.VMEM((8, d_model), F32),
            pltpu.VMEM((1, d_model), F32),
            pltpu.VMEM((NZ, 16, hw), BF16),
            pltpu.VMEM((NZ, 16, hw), BF16),
            pltpu.VMEM((NZ, 16, hw), BF16),
            pltpu.VMEM((ndp, 16, hw), BF16),
            pltpu.VMEM((2, pg, hw), BF16),
            pltpu.VMEM((2, 8 * NZ, hw), BF16),
            pltpu.VMEM((NZ, 8, pg), F32),
            pltpu.VMEM((NZ, 8, pg), F32),
            pltpu.VMEM((NZ, 8, 128), F32),
            pltpu.VMEM((NZ, NZ, pg), F32),
            pltpu.VMEM((NZ, fb // 128, 128), F32),
            pltpu.VMEM((NZ, fb // 128, 128), F32),
            pltpu.VMEM((NZ, 16, pg // 2), BF16),
            pltpu.VMEM((NZ, 16, hw), BF16),
            pltpu.VMEM((NZ, 16, hw), BF16),
            pltpu.VMEM((ndp, 16, hw), BF16),
            pltpu.VMEM((ndp, 16, hw), BF16),
            pltpu.VMEM((2, 2, ni // 2, rank, sw), BF16),
            pltpu.VMEM((rank, d_model), BF16),
            pltpu.VMEM((ni, rank, sw), BF16),
            pltpu.VMEM((ni, rank, sw), BF16),
            pltpu.VMEM((ni, rank, sw), BF16),
            pltpu.VMEM((ni, rank, sw), BF16),
            pltpu.VMEM((n_tiles, 8, 128), F32),
            pltpu.VMEM((ndp, 8, 128), F32),
            pltpu.VMEM((n_tiles, 8, 128), F32),
            pltpu.SemaphoreType.DMA((35,)),
            pltpu.SemaphoreType.DMA((ni,)),
            pltpu.SemaphoreType.DMA((9,)),
        ],
        compiler_params=pltpu.CompilerParams(
            collective_id=0, has_side_effects=True, vmem_limit_bytes=VMEM_BYTES
        ),
        name="contrastive_adapter",
    )(*(pltpu.with_memory_space_constraint(x, pltpu.HBM) for x in operands))
    return pl.pallas_call(
        store_kernel,
        out_shape=tuple(jax.ShapeDtypeStruct(r.shape, r.dtype) for r in results),
        in_specs=[vmem] * 4,
        out_specs=(hbm,) * 4,
        scratch_shapes=[pltpu.SemaphoreType.DMA((4,))],
        compiler_params=pltpu.CompilerParams(vmem_limit_bytes=2 * 1024 * 1024),
        name="store_results",
    )(*(pltpu.with_memory_space_constraint(r, pltpu.VMEM) for r in results))


def solution(mesh):
    wide = P("fsdp", "dp", None)
    in_specs = (
        wide, wide, P("fsdp", "dp"), P("fsdp", "dp"), wide, wide, P(), P(None, "fsdp"), P(None, "fsdp"),
    )
    out_specs = (wide, wide, P(None, "fsdp"), P(None, "fsdp"))
    body = functools.partial(per_device, mesh.shape["dp"], mesh.shape["fsdp"])
    return jax.shard_map(body, mesh=mesh, in_specs=in_specs, out_specs=out_specs, check_vma=False)
```

```python
import functools

import jax
import jax.numpy as jnp
from jax import lax
from jax.experimental import pallas as pl
from jax.experimental.pallas import tpu as pltpu
from jax.sharding import PartitionSpec as P

HB = 4
NZ = 8
SCALE = 50.0
EXTRA = 1.3862943611198906
EPS = 1e-06
VMEM_BYTES = 48 * 1024 * 1024
F32 = jnp.float32
BF16 = jnp.bfloat16
MESH = pl.DeviceIdType.MESH


def dot(a, b, ca=1, cb=0):
    return lax.dot_general(a, b, (((ca,), (cb,)), ((), ())), preferred_element_type=F32)


def landed(ref, sem):
    pltpu.make_async_copy(ref, ref, sem).wait()


def loop(low, high, body, unroll=1):
    def step(k, carry):
        body(k)
        return carry

    lax.fori_loop(low, high, step, 0, unroll=unroll)


def as_column(row):
    n = row.shape[1]
    wide = jnp.broadcast_to(row, (n, n))
    eye = lax.broadcasted_iota(jnp.int32, (n, n), 0) == lax.broadcasted_iota(jnp.int32, (n, n), 1)
    return jnp.sum(jnp.where(eye, wide, 0.0), axis=1, keepdims=True)


def as_row(column):
    n = column.shape[0]
    wide = jnp.broadcast_to(column, (n, n))
    eye = lax.broadcasted_iota(jnp.int32, (n, n), 0) == lax.broadcasted_iota(jnp.int32, (n, n), 1)
    return jnp.sum(jnp.where(eye, wide, 0.0), axis=0, keepdims=True)


def split_rows(ref):
    wide = ref[...].astype(F32)
    wide = wide.reshape((-1,) + wide.shape[-2:])
    n, _, w = wide.shape
    return [wide[:, 8 * h : 8 * h + 8, :].reshape(8 * n, w).astype(BF16) for h in (0, 1)]


def stacked(block):
    half = block.shape[-1] // 2
    return jnp.concatenate([block[:, :half], block[:, half:]], axis=0)


def farthest_first(ny, nz):
    offsets = [(dy, dz) for dy in range(ny) for dz in range(nz) if dy or dz]
    return sorted(offsets, key=lambda o: -(2 * min(o[0], ny - o[0]) + min(o[1], nz - o[1])))


def kernel(
    ndp, nf,
    q_hbm, p_hbm, pos_hbm, hard_hbm, gain_hbm, down_hbm, up_hbm, res_hbm, hid_hbm,
    qg_out, pg_out, gd_out, gu_out,
    q_in, p_in, pos_in, hard_in, gain_in, hid, res, normed, unit_q, unit_p, gain_row,
    eq, ep, rqa, rp, pmat, qmat, ps, rs, rtag, rsc, qc, rqc, rca, qs, rqr, pgs, rpg,
    rw, upf, sm, rmate, sa, ra, ty, tz_sum,
    sem, msem, in_sem,
):
    nz = NZ
    ny = ndp // nz
    ni = nf // 2
    rank, dw = down_hbm.shape
    uw = up_hbm.shape[1]
    sw = dw + uw
    d_model = unit_q.shape[1]
    fb = d_model // nz
    hw = fb // 2
    seq = res.shape[0]
    pg = ndp * 8

    d = lax.axis_index("dp")
    f = lax.axis_index("fsdp")
    y, z = lax.div(d, nz), lax.rem(d, nz)
    i0, core = lax.div(f, 2), lax.rem(f, 2)
    nx = ni // 2
    x, yl = lax.div(i0, 2), lax.rem(i0, 2)
    rq, rc = rqa.at[y], rca.at[y]
    mate = (d, 2 * i0 + 1 - core)

    def at_z(tz):
        return (y * nz + tz, f)

    def at_i(i):
        return (d, 2 * i + core)

    def send(src, dst, send_sem, recv_sem, device):
        pltpu.make_async_remote_copy(
            src_ref=src, dst_ref=dst, send_sem=send_sem, recv_sem=recv_sem,
            device_id=device, device_id_type=MESH,
        ).start()

    started = []
    own_w = rw.at[core, yl, x]
    loads = [
        pltpu.make_async_copy(src, dst, in_sem.at[k])
        for k, (src, dst) in enumerate((
            (p_hbm, p_in), (q_hbm, q_in),
            (down_hbm, own_w.at[:, pl.ds(0, dw)]), (up_hbm, own_w.at[:, pl.ds(dw, uw)]),
            (gain_hbm, gain_in), (pos_hbm, pos_in), (hard_hbm, hard_in),
            (hid_hbm.at[0], hid), (res_hbm.at[0], res),
        ))
    ]
    load_p, load_q, load_down, load_up, load_gain, load_pos, load_hard, load_hid, load_res = loads
    load_p.start()
    load_q.start()

    barrier = pltpu.get_barrier_semaphore()

    def greet(device):
        pl.semaphore_signal(barrier, inc=1, device_id=device, device_id_type=MESH)

    for dy, dz in farthest_first(ny, nz):
        greet((lax.rem(y + dy, ny) * nz + lax.rem(z + dz, nz), f))
    loop(1, ni, lambda k: greet(at_i(lax.rem(i0 + k, ni))))
    greet(mate)
    for load in loads[2:]:
        load.start()

    def unit_rows(ref, unit_ref, blocks):
        rows = ref[0].astype(F32)
        length = jnp.sqrt(jnp.sum(rows * rows, axis=1, keepdims=True) + EPS)
        unit = rows / length
        unit_ref[...] = unit
        for k in range(nz):
            blocks[k] = stacked(unit[:, k * fb : (k + 1) * fb]).astype(BF16)
        return length

    load_p.wait()
    len_p = unit_rows(p_in, unit_p, ep)
    load_q.wait()
    len_q = unit_rows(q_in, unit_q, eq)
    rp[d] = ep[z]
    rq[z] = eq[z]
    load_down.wait()
    load_up.wait()
    load_pos.wait()
    load_hard.wait()
    pos = as_column(pos_in[...].astype(F32))
    hard = as_column(hard_in[...].astype(F32))
    tag = jnp.where(lax.broadcasted_iota(jnp.int32, (8, 128), 1) < 64, pos[0:1], hard[0:1])
    rtag[z] = jnp.where(lax.broadcasted_iota(jnp.int32, (8, 128), 0) == z, tag, 0.0)

    pl.semaphore_wait(barrier, (ndp - 1) + (ni - 1) + 1)

    def send_p(dy, dz):
        tz = lax.rem(z + dz, nz)
        t = lax.rem(y + dy, ny) * nz + tz
        send(ep.at[tz], rp.at[d], sem.at[2], sem.at[3], (t, f))

    def send_q(k):
        tz = lax.rem(z + k, nz)
        send(eq.at[tz], rq.at[z], sem.at[4], sem.at[5], at_z(tz))
        send(rtag.at[z], rtag.at[z], sem.at[25], sem.at[26], at_z(tz))

    def send_w(k):
        send(own_w, own_w, sem.at[6], sem.at[7], at_i(2 * lax.rem(x + k, nx) + yl))

    for dy, dz in farthest_first(ny, nz):
        send_p(dy, dz)
    loop(1, nz, send_q)
    loop(1, nx, send_w)
    started += [
        (rtag.at[pl.ds(0, nz - 1)], sem.at[25]),
        (rp.at[pl.ds(0, ndp - 1)], sem.at[2]), (rq.at[pl.ds(0, nz - 1)], sem.at[4]),
    ]
    if nx > 1:
        started.append((rw.at[0, 0, pl.ds(0, nx - 1)], sem.at[6]))

    load_gain.wait()
    for k in range(gain_in.shape[0]):
        gain_row[0:1, 128 * k : 128 * (k + 1)] = gain_in[...].astype(F32)[k : k + 1, :]

    if nx > 1:
        landed(rw.at[core, yl, pl.ds(0, nx - 1)], sem.at[7])
    send(rw.at[core, yl], rw.at[core, yl], sem.at[10], sem.at[11], mate)
    started.append((rw.at[0, 0], sem.at[10]))
    load_hid.wait()

    def reduce_part(c, row, start):
        def step(k, acc):
            cols = pl.ds(pl.multiple_of((4 * k + 2 * row + c) * dw, 128), dw)
            return acc + dot(rw[c, row, k][:, :dw], hid[:, cols], 1, 1)

        return lax.fori_loop(0, nx, step, start, unroll=nx)

    reduced_t = reduce_part(core, yl, jnp.zeros((rank, seq), F32))
    landed(rw.at[1 - core, yl], sem.at[11])
    reduced_t = reduce_part(1 - core, yl, reduced_t)

    landed(rq.at[pl.ds(0, nz - 1)], sem.at[5])
    landed(rtag.at[pl.ds(0, nz - 1)], sem.at[26])
    landed(rp.at[pl.ds(0, ndp - 1)], sem.at[3])
    for h, half in enumerate(split_rows(rp)):
        pmat[h] = half
    for h, half in enumerate(split_rows(rq)):
        qmat[h] = half
    partial = dot(qmat[0], pmat[0], 1, 1) + dot(qmat[1], pmat[1], 1, 1)
    ps[...] = partial.reshape(nz, 8, pg)
    rs[z] = ps[z]
    for k in range(nz):
        rsc[z, k : k + 1, :] = ps[k, 0:1, :]

    def send_sc(k):
        send(rsc.at[z], rsc.at[z], sem.at[27], sem.at[28], at_z(lax.rem(z + k, nz)))

    loop(1, nz, send_sc)
    started.append((rsc.at[pl.ds(0, nz - 1)], sem.at[27]))

    send(rw.at[core, yl], rw.at[core, yl], sem.at[31], sem.at[32], at_i(2 * x + 1 - yl))
    started.append((rw.at[0, 0], sem.at[31]))
    landed(rw.at[core, 1 - yl], sem.at[32])
    send(rw.at[core, 1 - yl], rw.at[core, 1 - yl], sem.at[33], sem.at[34], mate)
    started.append((rw.at[0, 0], sem.at[33]))

    def at_y(k):
        return (lax.rem(y + k, ny) * nz + z, f)

    def send_yq(k):
        send(rqa.at[y], rqa.at[y], sem.at[35], sem.at[36], at_y(k))

    loop(1, ny, send_yq)
    started.append((rqa.at[pl.ds(0, ny - 1)], sem.at[35]))
    reduced_t = reduce_part(core, 1 - yl, reduced_t)

    def coefficients(products, positive, hard_block):
        ids = lax.broadcasted_iota(jnp.int32, products.shape, 1)
        blocks = lax.shift_right_logical(ids, 2).astype(F32)
        weights = jnp.exp(SCALE * products + jnp.where(blocks == hard_block, EXTRA, 0.0))
        soft = weights / jnp.sum(weights, axis=1, keepdims=True)
        return soft - jnp.where(ids.astype(F32) == positive, 1.0, 0.0)

    landed(rsc.at[pl.ds(0, nz - 1)], sem.at[28])
    tags = jnp.sum(rtag[...], axis=0)[:nz]
    first = coefficients(jnp.sum(rsc[...], axis=0), tags[:, 0:1], tags[:, 64:65]).astype(BF16)
    for h in range(2):
        term = SCALE * dot(first, pmat[h])
        for k in range(hw // 128):
            qc[:, h * (hw // 128) + k, :] = term[:, 128 * k : 128 * k + 128]
    rqc[z] = qc[z]

    def send_qc(k):
        tz = lax.rem(z + k, nz)
        send(qc.at[tz], rqc.at[z], sem.at[29], sem.at[30], at_z(tz))

    loop(1, nz, send_qc)
    started.append((rqc.at[pl.ds(0, nz - 1)], sem.at[29]))

    def send_s(k):
        tz = lax.rem(z + k, nz)
        send(ps.at[tz], rs.at[z], sem.at[8], sem.at[9], at_z(tz))

    loop(1, nz, send_s)
    started.append((rs.at[pl.ds(0, nz - 1)], sem.at[8]))

    landed(rw.at[1 - core, 1 - yl], sem.at[34])
    reduced_t = reduce_part(1 - core, 1 - yl, reduced_t).astype(BF16)
    for c in range(2):
        for row in range(2):
            for k in range(nx):
                at = (4 * k + 2 * row + c) * uw
                upf[:, at : at + uw] = rw[c, row, k][:, dw:]

    load_res.wait()
    cw = d_model // 4
    reduced = reduced_t.astype(F32).T.astype(BF16)

    def forward(j, squares):
        cols = pl.ds(pl.multiple_of(j * cw, 128), cw)
        part = res[:, cols].astype(F32) + 2.0 * dot(reduced, upf[:, cols])
        normed[:, cols] = part
        return squares + jnp.sum(part * part, axis=1, keepdims=True)

    squares = lax.fori_loop(0, d_model // cw, forward, jnp.zeros((seq, 1), F32))
    inv_root = 1.0 / jnp.sqrt(squares / d_model + EPS)
    inv_row = as_row(inv_root)

    def normalize(j, acc):
        cols = pl.ds(pl.multiple_of(j * cw, 128), cw)
        part = normed[:, cols] * inv_root
        normed[:, cols] = part
        high = part.astype(BF16)
        low = (part - high.astype(F32)).astype(BF16)
        return acc + (dot(upf[:, cols], high, 1, 1) + dot(upf[:, cols], low, 1, 1))

    normed_up = lax.fori_loop(0, d_model // cw, normalize, jnp.zeros((rank, seq), F32))

    def tangent(unit, raw, length):
        return (raw - unit * jnp.sum(unit * raw, axis=1, keepdims=True)) / length

    landed(rqc.at[pl.ds(0, nz - 1)], sem.at[30])
    first_raw = jnp.concatenate([rqc[k, c : c + 1, :] for k in range(nz) for c in range(fb // 128)], axis=1)
    upstream = tangent(unit_q[0:1, :], first_raw, len_q[0:1, :])

    grad_norm = gain_row[...] * upstream * (1.0 / seq)
    projected = jnp.sum(normed[...] * grad_norm, axis=1, keepdims=True) * (1.0 / d_model)
    up_grad = jnp.sum(upf[...].astype(F32) * grad_norm, axis=1, keepdims=True)
    grad_reduced_t = (2.0 * (up_grad - as_row(projected) * normed_up) * inv_row).astype(BF16)

    def terms_of(i, c):
        owner = 2 * i + c
        down_cols = pl.ds(pl.multiple_of(owner * dw, 128), dw)
        up_cols = pl.ds(pl.multiple_of(owner * uw, 128), uw)
        down_term = dot(grad_reduced_t, hid[:, down_cols])
        stream = ((gn[:, up_cols] - normed[:, up_cols] * projected) * inv_root).astype(BF16)
        return down_term, 2.0 * dot(reduced_t, stream)

    gn = gain_row
    gn[...] = grad_norm

    def for_mate(i):
        down_term, up_term = terms_of(i, 1 - core)
        sm[i, :, :dw] = down_term.astype(BF16)
        sm[i, :, dw:] = up_term.astype(BF16)
        send(sm.at[i], rmate.at[i], sem.at[18], msem.at[i], mate)

    def mate_step(k):
        for_mate(lax.rem(i0 + k, ni))

    loop(1, ni + 1, mate_step, unroll=ni)
    started.append((sm, sem.at[18]))

    landed(rs.at[pl.ds(0, nz - 1)], sem.at[9])
    coeffs = coefficients(jnp.sum(rs[...], axis=0), pos, hard)
    rc[z] = stacked(coeffs).astype(BF16)

    def send_c(k):
        send(rc.at[z], rc.at[z], sem.at[12], sem.at[13], at_z(lax.rem(z + k, nz)))

    loop(1, nz, send_c)
    started.append((rc.at[pl.ds(0, nz - 1)], sem.at[12]))

    def own_terms(i, out_ref, out_at):
        down_term, up_term = terms_of(i, core)
        landed(rmate.at[i], msem.at[i])
        other = rmate[i].astype(F32)
        out_ref[out_at, :, :dw] = (down_term + other[:, :dw]).astype(BF16)
        out_ref[out_at, :, dw:] = (up_term + other[:, dw:]).astype(BF16)

    def own_step(k):
        i = lax.rem(i0 + k, ni)
        own_terms(i, sa, i)
        send(sa.at[i], ra.at[i0], sem.at[19], sem.at[20], at_i(i))

    loop(1, ni, own_step, unroll=ni - 1)
    started.append((sa.at[pl.ds(0, ni - 1)], sem.at[19]))
    own_terms(i0, ra, i0)

    landed(rc.at[pl.ds(0, nz - 1)], sem.at[13])
    cmat = jnp.concatenate(split_rows(rc), axis=1)
    terms = [(SCALE * dot(cmat, pmat[h])).reshape(nz, 8, hw) for h in range(2)]
    qs[...] = jnp.concatenate(terms, axis=1).astype(BF16)
    rqr[z] = qs[z]

    def send_qr(k):
        tz = lax.rem(z + k, nz)
        send(qs.at[tz], rqr.at[z], sem.at[14], sem.at[15], at_z(tz))

    loop(1, nz, send_qr)
    started.append((rqr.at[pl.ds(0, nz - 1)], sem.at[14]))

    def send_yc(k):
        send(rca.at[y], rca.at[y], sem.at[37], sem.at[38], at_y(k))

    loop(1, ny, send_yc)
    started.append((rca.at[pl.ds(0, ny - 1)], sem.at[37]))

    landed(ra.at[pl.ds(0, ni - 1)], sem.at[20])
    ty[y] = jnp.sum(ra[...].astype(F32), axis=0).astype(BF16)

    def send_ty(k):
        send(ty.at[y], ty.at[y], sem.at[21], sem.at[22], (lax.rem(y + k, ny) * nz + z, f))

    loop(1, ny, send_ty, unroll=ny - 1)
    started.append((ty.at[pl.ds(0, ny - 1)], sem.at[21]))

    landed(rqa.at[pl.ds(0, ny - 1)], sem.at[36])
    landed(rca.at[pl.ds(0, ny - 1)], sem.at[38])
    call = jnp.concatenate(split_rows(rca), axis=1)
    terms = [(SCALE * dot(call, half, 0, 0)).reshape(ndp, 8, hw) for half in split_rows(rqa)]
    pgs[...] = jnp.concatenate(terms, axis=1).astype(BF16)
    rpg[z] = pgs[d]

    def send_pg(k):
        tz = lax.rem(z + k, nz)
        send(pgs.at[y * nz + tz], rpg.at[z], sem.at[16], sem.at[17], at_z(tz))

    loop(1, nz, send_pg)
    started.append((rpg.at[pl.ds(0, nz - 1)], sem.at[16]))

    landed(ty.at[pl.ds(0, ny - 1)], sem.at[22])
    tz_sum[z] = jnp.sum(ty[...].astype(F32), axis=0).astype(BF16)

    def send_tz(k):
        send(tz_sum.at[z], tz_sum.at[z], sem.at[23], sem.at[24], at_z(lax.rem(z + nz // 2 + k, nz)))

    for k in sorted(range(nz), key=lambda k: min((nz // 2 + k) % nz, nz - (nz // 2 + k) % nz), reverse=True)[:-1]:
        send_tz(k)
    started.append((tz_sum.at[pl.ds(0, nz - 1)], sem.at[23]))

    def unfolded(ref):
        wide = ref[...].astype(F32)
        return jnp.concatenate([wide[k, 8 * h : 8 * h + 8] for k in range(nz) for h in range(2)], axis=1)

    landed(rqr.at[pl.ds(0, nz - 1)], sem.at[15])
    qg_out[0] = tangent(unit_q[...], unfolded(rqr), len_q).astype(BF16)

    landed(rpg.at[pl.ds(0, nz - 1)], sem.at[17])
    pg_out[0] = tangent(unit_p[...], unfolded(rpg), len_p).astype(BF16)

    landed(tz_sum.at[pl.ds(0, nz - 1)], sem.at[24])
    total = jnp.sum(tz_sum[...].astype(F32), axis=0)
    gd_out[...] = total[:, :dw]
    gu_out[...] = total[:, dw:]

    for ref, left in started:
        landed(ref, left)


def store_kernel(*refs):
    sources, results, sem = refs[:4], refs[4:8], refs[8]
    stores = [pltpu.make_async_copy(sources[k], results[k], sem.at[k]) for k in range(4)]
    for store in stores:
        store.start()
    for store in stores:
        store.wait()


def per_device(ndp, nf, queries, passages, positives, hard_blocks, residual, hidden_act, gain, down_rows, up_rows):
    d_model = queries.shape[2]
    seq, hid = hidden_act.shape[1:]
    rank, dw = down_rows.shape
    uw = up_rows.shape[1]
    sw = dw + uw
    ni = nf // 2
    fb = d_model // NZ
    hw = fb // 2
    pg = ndp * 8
    hbm = pl.BlockSpec(memory_space=pltpu.HBM)
    vmem = pl.BlockSpec(memory_space=pltpu.VMEM)
    operands = (
        queries, passages, positives, hard_blocks, gain.reshape(d_model // 128, 128),
        down_rows, up_rows, residual, hidden_act,
    )
    results = pl.pallas_call(
        functools.partial(kernel, ndp, nf),
        out_shape=(
            pltpu.VMEM(queries.shape, BF16),
            pltpu.VMEM(passages.shape, BF16),
            pltpu.VMEM(down_rows.shape, F32),
            pltpu.VMEM(up_rows.shape, F32),
        ),
        in_specs=[hbm] * 9,
        out_specs=(vmem,) * 4,
        scratch_shapes=[
            pltpu.VMEM(queries.shape, BF16),
            pltpu.VMEM(passages.shape, BF16),
            pltpu.VMEM(positives.shape, jnp.int32),
            pltpu.VMEM(hard_blocks.shape, jnp.int32),
            pltpu.VMEM((d_model // 128, 128), BF16),
            pltpu.VMEM((seq, hid), BF16),
            pltpu.VMEM((seq, d_model), BF16),
            pltpu.VMEM((seq, d_model), F32),
            pltpu.VMEM((8, d_model), F32),
            pltpu.VMEM((8, d_model), F32),
            pltpu.VMEM((1, d_model), F32),
            pltpu.VMEM((NZ, 16, hw), BF16),
            pltpu.VMEM((NZ, 16, hw), BF16),
            pltpu.VMEM((ndp // NZ, NZ, 16, hw), BF16),
            pltpu.VMEM((ndp, 16, hw), BF16),
            pltpu.VMEM((2, pg, hw), BF16),
            pltpu.VMEM((2, 8 * NZ, hw), BF16),
            pltpu.VMEM((NZ, 8, pg), F32),
            pltpu.VMEM((NZ, 8, pg), F32),
            pltpu.VMEM((NZ, 8, 128), F32),
            pltpu.VMEM((NZ, NZ, pg), F32),
            pltpu.VMEM((NZ, fb // 128, 128), F32),
            pltpu.VMEM((NZ, fb // 128, 128), F32),
            pltpu.VMEM((ndp // NZ, NZ, 16, pg // 2), BF16),
            pltpu.VMEM((NZ, 16, hw), BF16),
            pltpu.VMEM((NZ, 16, hw), BF16),
            pltpu.VMEM((ndp, 16, hw), BF16),
            pltpu.VMEM((NZ, 16, hw), BF16),
            pltpu.VMEM((2, 2, ni // 2, rank, sw), BF16),
            pltpu.VMEM((rank, d_model), BF16),
            pltpu.VMEM((ni, rank, sw), BF16),
            pltpu.VMEM((ni, rank, sw), BF16),
            pltpu.VMEM((ni, rank, sw), BF16),
            pltpu.VMEM((ni, rank, sw), BF16),
            pltpu.VMEM((ndp // NZ, rank, sw), BF16),
            pltpu.VMEM((NZ, rank, sw), BF16),
            pltpu.SemaphoreType.DMA((39,)),
            pltpu.SemaphoreType.DMA((ni,)),
            pltpu.SemaphoreType.DMA((9,)),
        ],
        compiler_params=pltpu.CompilerParams(
            collective_id=0, has_side_effects=True, vmem_limit_bytes=VMEM_BYTES
        ),
        name="contrastive_adapter",
    )(*(pltpu.with_memory_space_constraint(x, pltpu.HBM) for x in operands))
    return pl.pallas_call(
        store_kernel,
        out_shape=tuple(jax.ShapeDtypeStruct(r.shape, r.dtype) for r in results),
        in_specs=[vmem] * 4,
        out_specs=(hbm,) * 4,
        scratch_shapes=[pltpu.SemaphoreType.DMA((4,))],
        compiler_params=pltpu.CompilerParams(vmem_limit_bytes=2 * 1024 * 1024),
        name="store_results",
    )(*(pltpu.with_memory_space_constraint(r, pltpu.VMEM) for r in results))


def solution(mesh):
    wide = P("fsdp", "dp", None)
    in_specs = (
        wide, wide, P("fsdp", "dp"), P("fsdp", "dp"), wide, wide, P(), P(None, "fsdp"), P(None, "fsdp"),
    )
    out_specs = (wide, wide, P(None, "fsdp"), P(None, "fsdp"))
    body = functools.partial(per_device, mesh.shape["dp"], mesh.shape["fsdp"])
    return jax.shard_map(body, mesh=mesh, in_specs=in_specs, out_specs=out_specs, check_vma=False)
```

```python
import functools

import jax
import jax.numpy as jnp
from jax import lax
from jax.experimental import pallas as pl
from jax.experimental.pallas import tpu as pltpu
from jax.sharding import PartitionSpec as P

HB = 4
NZ = 8
SCALE = 50.0
EXTRA = 1.3862943611198906
EPS = 1e-06
VMEM_BYTES = 48 * 1024 * 1024
F32 = jnp.float32
BF16 = jnp.bfloat16
MESH = pl.DeviceIdType.MESH


def dot(a, b, ca=1, cb=0):
    return lax.dot_general(a, b, (((ca,), (cb,)), ((), ())), preferred_element_type=F32)


def landed(ref, sem):
    pltpu.make_async_copy(ref, ref, sem).wait()


def loop(low, high, body, unroll=1):
    def step(k, carry):
        body(k)
        return carry

    lax.fori_loop(low, high, step, 0, unroll=unroll)


def as_column(row):
    n = row.shape[1]
    wide = jnp.broadcast_to(row, (n, n))
    eye = lax.broadcasted_iota(jnp.int32, (n, n), 0) == lax.broadcasted_iota(jnp.int32, (n, n), 1)
    return jnp.sum(jnp.where(eye, wide, 0.0), axis=1, keepdims=True)


def as_row(column):
    n = column.shape[0]
    wide = jnp.broadcast_to(column, (n, n))
    eye = lax.broadcasted_iota(jnp.int32, (n, n), 0) == lax.broadcasted_iota(jnp.int32, (n, n), 1)
    return jnp.sum(jnp.where(eye, wide, 0.0), axis=0, keepdims=True)


def split_rows(ref):
    wide = ref[...].astype(F32)
    wide = wide.reshape((-1,) + wide.shape[-2:])
    n, _, w = wide.shape
    return [wide[:, 8 * h : 8 * h + 8, :].reshape(8 * n, w).astype(BF16) for h in (0, 1)]


def stacked(block):
    half = block.shape[-1] // 2
    return jnp.concatenate([block[:, :half], block[:, half:]], axis=0)


def farthest_first(ny, nz):
    offsets = [(dy, dz) for dy in range(ny) for dz in range(nz) if dy or dz]
    return sorted(offsets, key=lambda o: -(2 * min(o[0], ny - o[0]) + min(o[1], nz - o[1])))


def far_z(nz):
    return sorted(range(1, nz), key=lambda k: -min(k, nz - k))


def kernel(
    ndp, nf,
    q_hbm, p_hbm, pos_hbm, hard_hbm, gain_hbm, down_hbm, up_hbm, res_hbm, hid_hbm,
    qg_out, pg_out, gd_out, gu_out,
    q_in, p_in, pos_in, hard_in, gain_in, hid, res, normed, unit_q, unit_p, gain_row,
    eq, ep, rqa, rp, pmat, qmat, ps, rs, rtag, rsc, qc, rqc, rc, cy, rcy, qs, rqr, pgs, rpg,
    rw, upf, sm, rmate, sa, ra, ty, tz_sum,
    sem, msem, in_sem,
):
    nz = NZ
    ny = ndp // nz
    ni = nf // 2
    rank, dw = down_hbm.shape
    uw = up_hbm.shape[1]
    sw = dw + uw
    d_model = unit_q.shape[1]
    fb = d_model // nz
    hw = fb // 2
    seq = res.shape[0]
    pg = ndp * 8
    pb = pg // ny

    d = lax.axis_index("dp")
    f = lax.axis_index("fsdp")
    y, z = lax.div(d, nz), lax.rem(d, nz)
    i0, core = lax.div(f, 2), lax.rem(f, 2)
    nx = ni // 2
    x, yl = lax.div(i0, 2), lax.rem(i0, 2)
    rq = rqa.at[y]
    mate = (d, 2 * i0 + 1 - core)

    def at_z(tz):
        return (y * nz + tz, f)

    def at_i(i):
        return (d, 2 * i + core)

    def send(src, dst, send_sem, recv_sem, device):
        pltpu.make_async_remote_copy(
            src_ref=src, dst_ref=dst, send_sem=send_sem, recv_sem=recv_sem,
            device_id=device, device_id_type=MESH,
        ).start()

    started = []
    own_w = rw.at[core, yl, x]
    loads = [
        pltpu.make_async_copy(src, dst, in_sem.at[k])
        for k, (src, dst) in enumerate((
            (p_hbm, p_in), (q_hbm, q_in),
            (down_hbm, own_w.at[:, pl.ds(0, dw)]), (up_hbm, own_w.at[:, pl.ds(dw, uw)]),
            (gain_hbm, gain_in), (pos_hbm, pos_in), (hard_hbm, hard_in),
            (hid_hbm.at[0], hid), (res_hbm.at[0], res),
        ))
    ]
    load_p, load_q, load_down, load_up, load_gain, load_pos, load_hard, load_hid, load_res = loads
    load_p.start()
    load_q.start()

    barrier = pltpu.get_barrier_semaphore()

    def greet(device):
        pl.semaphore_signal(barrier, inc=1, device_id=device, device_id_type=MESH)

    for dy, dz in farthest_first(ny, nz):
        greet((lax.rem(y + dy, ny) * nz + lax.rem(z + dz, nz), f))
    loop(1, ni, lambda k: greet(at_i(lax.rem(i0 + k, ni))))
    greet(mate)
    for load in loads[2:]:
        load.start()

    def unit_rows(ref, unit_ref, blocks):
        rows = ref[0].astype(F32)
        length = jnp.sqrt(jnp.sum(rows * rows, axis=1, keepdims=True) + EPS)
        unit = rows / length
        unit_ref[...] = unit
        for k in range(nz):
            blocks[k] = stacked(unit[:, k * fb : (k + 1) * fb]).astype(BF16)
        return length

    load_p.wait()
    len_p = unit_rows(p_in, unit_p, ep)
    load_q.wait()
    len_q = unit_rows(q_in, unit_q, eq)
    rp[d] = ep[z]
    rq[z] = eq[z]
    load_down.wait()
    load_up.wait()
    load_pos.wait()
    load_hard.wait()
    pos = as_column(pos_in[...].astype(F32))
    hard = as_column(hard_in[...].astype(F32))
    tag = jnp.where(lax.broadcasted_iota(jnp.int32, (8, 128), 1) < 64, pos[0:1], hard[0:1])
    rtag[z] = jnp.where(lax.broadcasted_iota(jnp.int32, (8, 128), 0) == z, tag, 0.0)

    pl.semaphore_wait(barrier, (ndp - 1) + (ni - 1) + 1)

    def send_p(dy, dz):
        tz = lax.rem(z + dz, nz)
        t = lax.rem(y + dy, ny) * nz + tz
        send(ep.at[tz], rp.at[d], sem.at[2], sem.at[3], (t, f))

    def send_q(k):
        tz = lax.rem(z + k, nz)
        send(eq.at[tz], rq.at[z], sem.at[4], sem.at[5], at_z(tz))
        send(rtag.at[z], rtag.at[z], sem.at[25], sem.at[26], at_z(tz))

    def send_w(k):
        send(own_w, own_w, sem.at[6], sem.at[7], at_i(2 * lax.rem(x + k, nx) + yl))

    for dy, dz in farthest_first(ny, nz):
        send_p(dy, dz)
    for k in far_z(nz):
        send_q(k)
    loop(1, nx, send_w)
    started += [
        (rtag.at[pl.ds(0, nz - 1)], sem.at[25]),
        (rp.at[pl.ds(0, ndp - 1)], sem.at[2]), (rq.at[pl.ds(0, nz - 1)], sem.at[4]),
    ]
    if nx > 1:
        started.append((rw.at[0, 0, pl.ds(0, nx - 1)], sem.at[6]))

    load_gain.wait()
    for k in range(gain_in.shape[0]):
        gain_row[0:1, 128 * k : 128 * (k + 1)] = gain_in[...].astype(F32)[k : k + 1, :]

    if nx > 1:
        landed(rw.at[core, yl, pl.ds(0, nx - 1)], sem.at[7])
    send(rw.at[core, yl], rw.at[core, yl], sem.at[10], sem.at[11], mate)
    started.append((rw.at[0, 0], sem.at[10]))
    load_hid.wait()

    def reduce_part(c, row, start):
        def step(k, acc):
            cols = pl.ds(pl.multiple_of((4 * k + 2 * row + c) * dw, 128), dw)
            return acc + dot(rw[c, row, k][:, :dw], hid[:, cols], 1, 1)

        return lax.fori_loop(0, nx, step, start, unroll=nx)

    reduced_t = reduce_part(core, yl, jnp.zeros((rank, seq), F32))
    landed(rw.at[1 - core, yl], sem.at[11])
    reduced_t = reduce_part(1 - core, yl, reduced_t)

    landed(rq.at[pl.ds(0, nz - 1)], sem.at[5])
    landed(rtag.at[pl.ds(0, nz - 1)], sem.at[26])
    landed(rp.at[pl.ds(0, ndp - 1)], sem.at[3])
    for h, half in enumerate(split_rows(rp)):
        pmat[h] = half
    for h, half in enumerate(split_rows(rq)):
        qmat[h] = half
    partial = dot(qmat[0], pmat[0], 1, 1) + dot(qmat[1], pmat[1], 1, 1)
    ps[...] = partial.reshape(nz, 8, pg)
    rs[z] = ps[z]
    for k in range(nz):
        rsc[z, k : k + 1, :] = ps[k, 0:1, :]

    def send_sc(k):
        send(rsc.at[z], rsc.at[z], sem.at[27], sem.at[28], at_z(lax.rem(z + k, nz)))

    for k in far_z(nz):
        send_sc(k)
    started.append((rsc.at[pl.ds(0, nz - 1)], sem.at[27]))

    send(rw.at[core, yl], rw.at[core, yl], sem.at[31], sem.at[32], at_i(2 * x + 1 - yl))
    started.append((rw.at[0, 0], sem.at[31]))
    landed(rw.at[core, 1 - yl], sem.at[32])
    send(rw.at[core, 1 - yl], rw.at[core, 1 - yl], sem.at[33], sem.at[34], mate)
    started.append((rw.at[0, 0], sem.at[33]))

    def at_y(k):
        return (lax.rem(y + k, ny) * nz + z, f)

    def send_yq(k):
        send(rqa.at[y], rqa.at[y], sem.at[35], sem.at[36], at_y(k))

    loop(1, ny, send_yq)
    started.append((rqa.at[pl.ds(0, ny - 1)], sem.at[35]))
    reduced_t = reduce_part(core, 1 - yl, reduced_t)

    def coefficients(products, positive, hard_block):
        ids = lax.broadcasted_iota(jnp.int32, products.shape, 1)
        blocks = lax.shift_right_logical(ids, 2).astype(F32)
        weights = jnp.exp(SCALE * products + jnp.where(blocks == hard_block, EXTRA, 0.0))
        soft = weights / jnp.sum(weights, axis=1, keepdims=True)
        return soft - jnp.where(ids.astype(F32) == positive, 1.0, 0.0)

    landed(rsc.at[pl.ds(0, nz - 1)], sem.at[28])
    tags = jnp.sum(rtag[...], axis=0)[:nz]
    first = coefficients(jnp.sum(rsc[...], axis=0), tags[:, 0:1], tags[:, 64:65]).astype(BF16)
    for h in range(2):
        term = SCALE * dot(first, pmat[h])
        for k in range(hw // 128):
            qc[:, h * (hw // 128) + k, :] = term[:, 128 * k : 128 * k + 128]
    rqc[z] = qc[z]

    def send_qc(k):
        tz = lax.rem(z + k, nz)
        send(qc.at[tz], rqc.at[z], sem.at[29], sem.at[30], at_z(tz))

    for k in far_z(nz):
        send_qc(k)
    started.append((rqc.at[pl.ds(0, nz - 1)], sem.at[29]))

    def send_s(k):
        tz = lax.rem(z + k, nz)
        send(ps.at[tz], rs.at[z], sem.at[8], sem.at[9], at_z(tz))

    for k in far_z(nz):
        send_s(k)
    started.append((rs.at[pl.ds(0, nz - 1)], sem.at[8]))

    landed(rw.at[1 - core, 1 - yl], sem.at[34])
    reduced_t = reduce_part(1 - core, 1 - yl, reduced_t).astype(BF16)
    for c in range(2):
        for row in range(2):
            for k in range(nx):
                at = (4 * k + 2 * row + c) * uw
                upf[:, at : at + uw] = rw[c, row, k][:, dw:]

    load_res.wait()
    cw = d_model // 4
    reduced = reduced_t.astype(F32).T.astype(BF16)

    def forward(j, squares):
        cols = pl.ds(pl.multiple_of(j * cw, 128), cw)
        part = res[:, cols].astype(F32) + 2.0 * dot(reduced, upf[:, cols])
        normed[:, cols] = part
        return squares + jnp.sum(part * part, axis=1, keepdims=True)

    squares = lax.fori_loop(0, d_model // cw, forward, jnp.zeros((seq, 1), F32))
    inv_root = 1.0 / jnp.sqrt(squares / d_model + EPS)
    inv_row = as_row(inv_root)

    def normalize(j, acc):
        cols = pl.ds(pl.multiple_of(j * cw, 128), cw)
        part = normed[:, cols] * inv_root
        normed[:, cols] = part
        high = part.astype(BF16)
        low = (part - high.astype(F32)).astype(BF16)
        return acc + (dot(upf[:, cols], high, 1, 1) + dot(upf[:, cols], low, 1, 1))

    normed_up = lax.fori_loop(0, d_model // cw, normalize, jnp.zeros((rank, seq), F32))

    def tangent(unit, raw, length):
        return (raw - unit * jnp.sum(unit * raw, axis=1, keepdims=True)) / length

    landed(rqc.at[pl.ds(0, nz - 1)], sem.at[30])
    first_raw = jnp.concatenate([rqc[k, c : c + 1, :] for k in range(nz) for c in range(fb // 128)], axis=1)
    upstream = tangent(unit_q[0:1, :], first_raw, len_q[0:1, :])

    grad_norm = gain_row[...] * upstream * (1.0 / seq)
    projected = jnp.sum(normed[...] * grad_norm, axis=1, keepdims=True) * (1.0 / d_model)
    up_grad = jnp.sum(upf[...].astype(F32) * grad_norm, axis=1, keepdims=True)
    grad_reduced_t = (2.0 * (up_grad - as_row(projected) * normed_up) * inv_row).astype(BF16)

    def terms_of(i, c):
        owner = 2 * i + c
        down_cols = pl.ds(pl.multiple_of(owner * dw, 128), dw)
        up_cols = pl.ds(pl.multiple_of(owner * uw, 128), uw)
        down_term = dot(grad_reduced_t, hid[:, down_cols])
        stream = ((gn[:, up_cols] - normed[:, up_cols] * projected) * inv_root).astype(BF16)
        return down_term, 2.0 * dot(reduced_t, stream)

    gn = gain_row
    gn[...] = grad_norm

    def for_mate(i):
        down_term, up_term = terms_of(i, 1 - core)
        sm[i, :, :dw] = down_term.astype(BF16)
        sm[i, :, dw:] = up_term.astype(BF16)
        send(sm.at[i], rmate.at[i], sem.at[18], msem.at[i], mate)

    def owner_of(dx, dyl):
        return 2 * lax.rem(x + dx, nx) + lax.rem(yl + dyl, 2)

    order = sorted(((dx, dyl) for dx in range(nx) for dyl in range(2)), key=lambda o: -(min(o[0], nx - o[0]) + o[1]))
    for dx, dyl in order:
        for_mate(owner_of(dx, dyl))
    started.append((sm, sem.at[18]))

    landed(rs.at[pl.ds(0, nz - 1)], sem.at[9])
    coeffs = coefficients(jnp.sum(rs[...], axis=0), pos, hard)
    rc[z] = stacked(coeffs).astype(BF16)

    def send_c(k):
        send(rc.at[z], rc.at[z], sem.at[12], sem.at[13], at_z(lax.rem(z + k, nz)))

    for k in far_z(nz):
        send_c(k)
    started.append((rc.at[pl.ds(0, nz - 1)], sem.at[12]))

    def own_terms(i, out_ref, out_at):
        down_term, up_term = terms_of(i, core)
        landed(rmate.at[i], msem.at[i])
        other = rmate[i].astype(F32)
        out_ref[out_at, :, :dw] = (down_term + other[:, :dw]).astype(BF16)
        out_ref[out_at, :, dw:] = (up_term + other[:, dw:]).astype(BF16)

    for dx, dyl in order[:-1]:
        i = owner_of(dx, dyl)
        own_terms(i, sa, i)
        send(sa.at[i], ra.at[i0], sem.at[19], sem.at[20], at_i(i))
    started.append((sa.at[pl.ds(0, ni - 1)], sem.at[19]))
    own_terms(i0, ra, i0)

    landed(rc.at[pl.ds(0, nz - 1)], sem.at[13])
    cmat = jnp.concatenate(split_rows(rc), axis=1)

    wide_c = cmat.astype(F32)
    half_rows = 4 * nz
    for k in range(ny):
        block = wide_c[:, pb * k : pb * k + pb]
        cy[k] = jnp.concatenate([block[:half_rows], block[half_rows:]], axis=1).astype(BF16)
    rcy[y] = cy[y]

    def send_yc(k):
        send(cy.at[lax.rem(y + k, ny)], rcy.at[y], sem.at[37], sem.at[38], at_y(k))

    loop(1, ny, send_yc)
    started.append((rcy.at[pl.ds(0, ny - 1)], sem.at[37]))
    terms = [(SCALE * dot(cmat, pmat[h])).reshape(nz, 8, hw) for h in range(2)]
    qs[...] = jnp.concatenate(terms, axis=1).astype(BF16)
    rqr[z] = qs[z]

    def send_qr(k):
        tz = lax.rem(z + k, nz)
        send(qs.at[tz], rqr.at[z], sem.at[14], sem.at[15], at_z(tz))

    for k in far_z(nz):
        send_qr(k)
    started.append((rqr.at[pl.ds(0, nz - 1)], sem.at[14]))

    landed(ra.at[pl.ds(0, ni - 1)], sem.at[20])
    ty[y] = jnp.sum(ra[...].astype(F32), axis=0).astype(BF16)

    def send_ty(k):
        send(ty.at[y], ty.at[y], sem.at[21], sem.at[22], (lax.rem(y + k, ny) * nz + z, f))

    loop(1, ny, send_ty, unroll=ny - 1)
    started.append((ty.at[pl.ds(0, ny - 1)], sem.at[21]))

    landed(rqa.at[pl.ds(0, ny - 1)], sem.at[36])
    landed(rcy.at[pl.ds(0, ny - 1)], sem.at[38])
    wide_c = rcy[...].astype(F32)
    blocks_c = [wide_c[k][:, pb * h : pb * h + pb] for k in range(ny) for h in range(2)]
    call = jnp.concatenate(blocks_c, axis=0).astype(BF16)
    terms = [(SCALE * dot(call, half, 0, 0)).reshape(nz, 8, hw) for half in split_rows(rqa)]
    pgs[...] = jnp.concatenate(terms, axis=1).astype(BF16)
    rpg[z] = pgs[z]

    def send_pg(k):
        tz = lax.rem(z + k, nz)
        send(pgs.at[tz], rpg.at[z], sem.at[16], sem.at[17], at_z(tz))

    for k in far_z(nz):
        send_pg(k)
    started.append((rpg.at[pl.ds(0, nz - 1)], sem.at[16]))

    landed(ty.at[pl.ds(0, ny - 1)], sem.at[22])
    tz_sum[z] = jnp.sum(ty[...].astype(F32), axis=0).astype(BF16)

    def send_tz(k):
        send(tz_sum.at[z], tz_sum.at[z], sem.at[23], sem.at[24], at_z(lax.rem(z + k, nz)))

    for k in far_z(nz):
        send_tz(k)
    started.append((tz_sum.at[pl.ds(0, nz - 1)], sem.at[23]))

    def unfolded(ref):
        wide = ref[...].astype(F32)
        return jnp.concatenate([wide[k, 8 * h : 8 * h + 8] for k in range(nz) for h in range(2)], axis=1)

    landed(rqr.at[pl.ds(0, nz - 1)], sem.at[15])
    qg_out[0] = tangent(unit_q[...], unfolded(rqr), len_q).astype(BF16)

    landed(rpg.at[pl.ds(0, nz - 1)], sem.at[17])
    pg_out[0] = tangent(unit_p[...], unfolded(rpg), len_p).astype(BF16)

    landed(tz_sum.at[pl.ds(0, nz - 1)], sem.at[24])
    total = jnp.sum(tz_sum[...].astype(F32), axis=0)
    gd_out[...] = total[:, :dw]
    gu_out[...] = total[:, dw:]

    for ref, left in started:
        landed(ref, left)


def store_kernel(*refs):
    sources, results, sem = refs[:4], refs[4:8], refs[8]
    stores = [pltpu.make_async_copy(sources[k], results[k], sem.at[k]) for k in range(4)]
    for store in stores:
        store.start()
    for store in stores:
        store.wait()


def per_device(ndp, nf, queries, passages, positives, hard_blocks, residual, hidden_act, gain, down_rows, up_rows):
    d_model = queries.shape[2]
    seq, hid = hidden_act.shape[1:]
    rank, dw = down_rows.shape
    uw = up_rows.shape[1]
    sw = dw + uw
    ni = nf // 2
    fb = d_model // NZ
    hw = fb // 2
    pg = ndp * 8
    hbm = pl.BlockSpec(memory_space=pltpu.HBM)
    vmem = pl.BlockSpec(memory_space=pltpu.VMEM)
    operands = (
        queries, passages, positives, hard_blocks, gain.reshape(d_model // 128, 128),
        down_rows, up_rows, residual, hidden_act,
    )
    results = pl.pallas_call(
        functools.partial(kernel, ndp, nf),
        out_shape=(
            pltpu.VMEM(queries.shape, BF16),
            pltpu.VMEM(passages.shape, BF16),
            pltpu.VMEM(down_rows.shape, F32),
            pltpu.VMEM(up_rows.shape, F32),
        ),
        in_specs=[hbm] * 9,
        out_specs=(vmem,) * 4,
        scratch_shapes=[
            pltpu.VMEM(queries.shape, BF16),
            pltpu.VMEM(passages.shape, BF16),
            pltpu.VMEM(positives.shape, jnp.int32),
            pltpu.VMEM(hard_blocks.shape, jnp.int32),
            pltpu.VMEM((d_model // 128, 128), BF16),
            pltpu.VMEM((seq, hid), BF16),
            pltpu.VMEM((seq, d_model), BF16),
            pltpu.VMEM((seq, d_model), F32),
            pltpu.VMEM((8, d_model), F32),
            pltpu.VMEM((8, d_model), F32),
            pltpu.VMEM((1, d_model), F32),
            pltpu.VMEM((NZ, 16, hw), BF16),
            pltpu.VMEM((NZ, 16, hw), BF16),
            pltpu.VMEM((ndp // NZ, NZ, 16, hw), BF16),
            pltpu.VMEM((ndp, 16, hw), BF16),
            pltpu.VMEM((2, pg, hw), BF16),
            pltpu.VMEM((2, 8 * NZ, hw), BF16),
            pltpu.VMEM((NZ, 8, pg), F32),
            pltpu.VMEM((NZ, 8, pg), F32),
            pltpu.VMEM((NZ, 8, 128), F32),
            pltpu.VMEM((NZ, NZ, pg), F32),
            pltpu.VMEM((NZ, fb // 128, 128), F32),
            pltpu.VMEM((NZ, fb // 128, 128), F32),
            pltpu.VMEM((NZ, 16, pg // 2), BF16),
            pltpu.VMEM((ndp // NZ, 4 * NZ, 2 * pg // (ndp // NZ)), BF16),
            pltpu.VMEM((ndp // NZ, 4 * NZ, 2 * pg // (ndp // NZ)), BF16),
            pltpu.VMEM((NZ, 16, hw), BF16),
            pltpu.VMEM((NZ, 16, hw), BF16),
            pltpu.VMEM((NZ, 16, hw), BF16),
            pltpu.VMEM((NZ, 16, hw), BF16),
            pltpu.VMEM((2, 2, ni // 2, rank, sw), BF16),
            pltpu.VMEM((rank, d_model), BF16),
            pltpu.VMEM((ni, rank, sw), BF16),
            pltpu.VMEM((ni, rank, sw), BF16),
            pltpu.VMEM((ni, rank, sw), BF16),
            pltpu.VMEM((ni, rank, sw), BF16),
            pltpu.VMEM((ndp // NZ, rank, sw), BF16),
            pltpu.VMEM((NZ, rank, sw), BF16),
            pltpu.SemaphoreType.DMA((39,)),
            pltpu.SemaphoreType.DMA((ni,)),
            pltpu.SemaphoreType.DMA((9,)),
        ],
        compiler_params=pltpu.CompilerParams(
            collective_id=0, has_side_effects=True, vmem_limit_bytes=VMEM_BYTES
        ),
        name="contrastive_adapter",
    )(*(pltpu.with_memory_space_constraint(x, pltpu.HBM) for x in operands))
    return pl.pallas_call(
        store_kernel,
        out_shape=tuple(jax.ShapeDtypeStruct(r.shape, r.dtype) for r in results),
        in_specs=[vmem] * 4,
        out_specs=(hbm,) * 4,
        scratch_shapes=[pltpu.SemaphoreType.DMA((4,))],
        compiler_params=pltpu.CompilerParams(vmem_limit_bytes=2 * 1024 * 1024),
        name="store_results",
    )(*(pltpu.with_memory_space_constraint(r, pltpu.VMEM) for r in results))


def solution(mesh):
    wide = P("fsdp", "dp", None)
    in_specs = (
        wide, wide, P("fsdp", "dp"), P("fsdp", "dp"), wide, wide, P(), P(None, "fsdp"), P(None, "fsdp"),
    )
    out_specs = (wide, wide, P(None, "fsdp"), P(None, "fsdp"))
    body = functools.partial(per_device, mesh.shape["dp"], mesh.shape["fsdp"])
    return jax.shard_map(body, mesh=mesh, in_specs=in_specs, out_specs=out_specs, check_vma=False)
```
